512 devices in a mesh: cube: 64 (over z, x_lo, core), sub: 8 (over y, x_hi).
Axes of the slice: x: 4 (x_hi: 2, x_lo: 2; x = x_hi * 2 + x_lo), y: 4, z: 16, core: 2. Of those that a mesh axis runs over, the one named last changes fastest.
Arguments:
- leaf_fronts: bfloat16 [16384, 2048], P('cube', 'sub'), may hold values from -8 to 8, as said below
- pivot_entries: bfloat16 [7, 256, 256], replicated, may hold values from -8 to 8, as said below
- pivot_inverse: bfloat16 [15, 2, 128, 128], replicated, as said below
- block_map_one: int32 [4, 2, 14], replicated, may hold values from 0 to 31, as said below
- block_map_two: int32 [2, 2, 30], replicated, may hold values from 0 to 63, as said below
- block_map_top: int32 [1, 2, 62], replicated, may hold values from 0 to 127, as said below
Outputs:
- top_front: bfloat16 [16384, 16384], P('cube', 'sub')
The draws below stay inside these ranges and needn't reach their ends.
Inputs may be any that keep to these rules, and one draw needn't show every extreme that they name: `leaf_fronts`: each front is symmetric in natural order. `pivot_entries`: each pivot block pair is symmetric. `pivot_inverse`: each inverse is symmetric. `block_map_one`: for each front and child the entries are distinct, and entry i is congruent to i + 2 modulo 8; parent block 1 receives a block of the second child. `block_map_two`: for each front and child the entries are distinct, and entry i is congruent to i + 2 modulo 2 * 8; parent block 1 receives a block of the second child. `block_map_top`: for each child the entries are distinct, and entry i is congruent to i + 2 modulo 4 * 8; parent block 1 receives a block of the second child.
All inputs are finite; a program needn't handle non-finite values.
Results may differ from the reference program's by a relative error of at most 0.025.
Values may be sent and summed in bfloat16 or wider, within the bound.
No kernel may reach another device: no remote copies, remote signals or barrier semaphores. Data moves between devices by JAX's collectives and lax.ppermute only.
A program may use at most 64 MiB of HBM per device.

```python
import math
import jax
import jax.numpy as jnp
from jax import lax

BLOCK = 128
ROW_BLOCKS = 2
LEAF_GROUP = 8
LEAF_BLOCKS = 16
N_CUBE = 64
N_SUB = 8


def arrange(natural, group_size):
    front_count = natural.shape[0]
    order_size = natural.shape[1]
    blocks = order_size // BLOCK
    shaped = natural.reshape(front_count, blocks // group_size, group_size, BLOCK, blocks, N_SUB, BLOCK // N_SUB)
    shaped = shaped.transpose(0, 2, 1, 3, 5, 4, 6)
    return shaped.reshape(front_count * order_size, order_size)


def draw_maps(key, front_count, child_group):
    candidates = 2 * ROW_BLOCKS
    scores = jax.random.randint(key, (front_count, 2, child_group, candidates), 0, 1 << 20) * candidates
    scores = scores + jnp.arange(candidates, dtype=jnp.int32)
    scores = scores.at[:, 0, child_group - 1, candidates - 1].set(-1)
    scores = scores.at[:, 0, child_group - 1, 0].set(-2)
    scores = scores.at[:, 1, 0, 1].set(-2)
    scores = scores.at[:, 1, 0, 0].set(-1)
    scores = scores.at[:, 1, 1, 1].set(-2)
    scores = scores.at[:, 1, 1, 0].set(-1)
    ranking = jnp.argsort(scores, axis=-1).astype(jnp.int32)
    child_rows = jnp.arange(2, ROW_BLOCKS * child_group, dtype=jnp.int32)
    residue = child_rows % child_group
    turn_index = child_rows // child_group
    chosen = ranking[:, :, residue, turn_index]
    return (residue[None, None, :] + child_group * chosen).astype(jnp.int32)


def draw_leaf_fronts(key, part):
    key = jax.random.fold_in(key, 1)
    order_size = LEAF_BLOCKS * BLOCK
    raw_values = jax.random.normal(key, (8, order_size, order_size), jnp.float32)
    symmetric = (raw_values + jnp.swapaxes(raw_values, 1, 2)) * 0.7071
    return arrange(symmetric, LEAF_GROUP).astype(jnp.bfloat16)


def draw_pivot_entries(key, part):
    key = jax.random.fold_in(key, 3)
    raw_values = jax.random.normal(key, (7, 2 * BLOCK, 2 * BLOCK), jnp.float32)
    symmetric = (raw_values + jnp.swapaxes(raw_values, 1, 2)) * 0.7071
    coupling = jax.random.uniform(jax.random.fold_in(key, 6), (7, BLOCK, BLOCK), jnp.float32, -6.0, 6.0)
    symmetric = symmetric.at[:, BLOCK:, :BLOCK].set(coupling)
    symmetric = symmetric.at[:, :BLOCK, BLOCK:].set(jnp.swapaxes(coupling, 1, 2))
    return jnp.clip(symmetric, -8.0, 8.0).astype(jnp.bfloat16)


def draw_pivot_inverse(key, part):
    key = jax.random.fold_in(key, 4)
    diagonal_part = jnp.exp(jax.random.uniform(key, (15, 2, BLOCK), jnp.float32, 0.0, math.log(4.0)))
    coupling = jax.random.normal(jax.random.fold_in(key, 5), (15, 2, BLOCK, BLOCK), jnp.float32)
    coupling = (coupling + jnp.swapaxes(coupling, 2, 3)) * 0.7071 * 0.05
    identity = jnp.eye(BLOCK, dtype=jnp.float32)
    return ((coupling + identity * diagonal_part[:, :, :, None]) / BLOCK).astype(jnp.bfloat16)


def draw_block_map_one(key, part):
    key = jax.random.fold_in(key, 11)
    return draw_maps(key, 4, LEAF_GROUP)


def draw_block_map_two(key, part):
    key = jax.random.fold_in(key, 12)
    return draw_maps(key, 2, 2 * LEAF_GROUP)


def draw_block_map_top(key, part):
    key = jax.random.fold_in(key, 13)
    return draw_maps(key, 1, 4 * LEAF_GROUP)


def setup_inputs(seed: int = 0) -> dict:
    streams_of = jax.random.split(jax.random.key(seed), 7)
    return {
        "leaf_fronts": draw_leaf_fronts(jax.random.fold_in(streams_of[6], 71), 0),
        "pivot_entries": draw_pivot_entries(jax.random.fold_in(streams_of[6], 71), 0),
        "pivot_inverse": draw_pivot_inverse(jax.random.fold_in(streams_of[6], 71), 0),
        "block_map_one": draw_block_map_one(jax.random.fold_in(streams_of[6], 71), 0),
        "block_map_two": draw_block_map_two(jax.random.fold_in(streams_of[6], 71), 0),
        "block_map_top": draw_block_map_top(jax.random.fold_in(streams_of[6], 71), 0),
    }


def to_layout(natural, group_size):
    front_count = natural.shape[0]
    order_size = natural.shape[1]
    blocks = order_size // BLOCK
    shaped = natural.reshape(front_count, blocks // group_size, group_size, BLOCK, blocks, N_SUB, BLOCK // N_SUB)
    shaped = shaped.transpose(0, 2, 1, 3, 5, 4, 6)
    return shaped.reshape(front_count * order_size, order_size)


def from_layout(stored, group_size, blocks):
    order_size = blocks * BLOCK
    front_count = stored.shape[0] // order_size
    shaped = stored.reshape(front_count, group_size, blocks // group_size, BLOCK, N_SUB, blocks, BLOCK // N_SUB)
    shaped = shaped.transpose(0, 2, 1, 3, 5, 4, 6)
    return shaped.reshape(front_count, order_size, order_size)


def factor_front(front_tile, inverses):
    for panel_idx in range(2):
        column = front_tile[:, panel_idx * BLOCK:(panel_idx + 1) * BLOCK].astype(jnp.bfloat16)
        scaled = jnp.dot(column, inverses[panel_idx], preferred_element_type=jnp.float32).astype(jnp.bfloat16)
        front_tile = front_tile - jnp.dot(scaled, column.T, preferred_element_type=jnp.float32)
    return front_tile


def extend_add(parent, child, block_list):
    inner = child[2 * BLOCK:, 2 * BLOCK:].astype(jnp.float32)
    offsets = jnp.arange(BLOCK, dtype=jnp.int32)
    index_list = (block_list.astype(jnp.int32)[:, None] * BLOCK + offsets[None, :]).reshape(-1).astype(jnp.int32)
    return parent.at[index_list[:, None], index_list[None, :]].add(inner)


def reference(leaf_fronts, pivot_entries, pivot_inverse, block_map_one, block_map_two, block_map_top):
    map_tables = (block_map_one, block_map_two, block_map_top)
    natural = from_layout(leaf_fronts, LEAF_GROUP, LEAF_BLOCKS)
    results = []
    for front_idx in range(8):
        factored = factor_front(natural[front_idx].astype(jnp.float32), pivot_inverse[front_idx])
        results.append(factored.astype(jnp.bfloat16))
    for level_idx in range(1, 4):
        front_count = 8 >> level_idx
        blocks = LEAF_BLOCKS << level_idx
        base_inverse = 16 - (16 >> level_idx)
        base_pivot = 8 - (16 >> level_idx)
        next_results = []
        for front_idx in range(front_count):
            parent = jnp.zeros((blocks * BLOCK, blocks * BLOCK), jnp.float32)
            parent = parent.at[:2 * BLOCK, :2 * BLOCK].add(pivot_entries[base_pivot + front_idx].astype(jnp.float32))
            for child_idx in range(2):
                parent = extend_add(parent, results[2 * front_idx + child_idx], map_tables[level_idx - 1][front_idx, child_idx])
            stored = lax.optimization_barrier(parent.astype(jnp.bfloat16))
            factored = factor_front(stored.astype(jnp.float32), pivot_inverse[base_inverse + front_idx])
            next_results.append(factored.astype(jnp.bfloat16))
        results = next_results
    return to_layout(results[0][None], N_CUBE)
```

```python
import jax
import jax.numpy as jnp
from jax import lax
from jax.sharding import Mesh, PartitionSpec as P

BLOCK = 128
F32 = jnp.float32
BF16 = jnp.bfloat16


def dot(lhs, rhs):
    return jnp.dot(lhs, rhs, preferred_element_type=F32)


def dot_tn(lhs, rhs):
    return lax.dot_general(lhs, rhs, (((0,), (0,)), ((), ())), preferred_element_type=F32)


def panels(first, second, inverses, row_one):
    scaled_zero = dot(inverses[0], first).astype(BF16)
    coupling = first[:, row_one : row_one + BLOCK]
    col_one = (second.astype(F32) - dot_tn(coupling, scaled_zero)).astype(BF16)
    scaled_one = dot(inverses[1], col_one).astype(BF16)
    columns = jnp.concatenate([first, col_one], 0)
    scaled = jnp.concatenate([scaled_zero, scaled_one], 0)
    return columns, scaled


def placement(block_list, parent_blocks, subcols):
    spots = (block_list[:, None] * subcols + jnp.arange(subcols, dtype=jnp.int32)).reshape(-1)
    spots = jnp.concatenate([jnp.full((2 * subcols,), -1, jnp.int32), spots])
    lanes = jnp.arange(parent_blocks * subcols, dtype=jnp.int32)
    return (spots[:, None] == lanes[None, :]).astype(BF16)


def find(block_list, wanted):
    hits = block_list == wanted
    places = jnp.arange(2, block_list.shape[0] + 2, dtype=jnp.int32)
    return jnp.where(jnp.any(hits), jnp.sum(jnp.where(hits, places, 0)), -1)


def gather_ring(payload, k, count):
    parts = [(payload, k)]
    ahead = behind = payload
    up = [(i, (i + 1) % count) for i in range(count)]
    down = [(i, (i - 1) % count) for i in range(count)]
    for step in range(1, count // 2 + 1):
        ahead = lax.ppermute(ahead, "k", up)
        parts.append((ahead, (k - step) % count))
        if step < count // 2:
            behind = lax.ppermute(behind, "k", down)
            parts.append((behind, (k + step) % count))
    whole = jnp.zeros((count,) + payload.shape, payload.dtype)
    for part, spot in parts:
        whole = lax.dynamic_update_slice_in_dim(whole, part[None], spot, 0)
    return whole


def leaf_stage(leaf, inverses, zl, xl, c, u, s):
    tile = leaf
    spread = jnp.where(xl == 0, tile, lax.ppermute(tile, "xl", [(0, 1)]))
    spread = jnp.where(zl == 0, spread, lax.ppermute(spread, "zl", [(0, 1)]))
    other = lax.ppermute(spread, "c", [(0, 1), (1, 0)])
    even = jnp.where(c == 0, spread, other)
    odd = jnp.where(c == 0, other, spread)
    piece = jnp.concatenate(
        [
            tile[:, :32],
            odd[:BLOCK, :32],
            even[BLOCK:, :32],
            odd[BLOCK:, :32],
            even[BLOCK:, 128:160],
            odd[BLOCK:, 128:160],
        ],
        0,
    ).T
    got = lax.all_to_all(jnp.broadcast_to(piece[None], (8,) + piece.shape), "sub", 0, 0, tiled=True)
    got = got.reshape(8, 2, 16, 896).transpose(1, 0, 2, 3).reshape(2, BLOCK, 896)
    first = jnp.concatenate([even[:BLOCK], got[0, :, :640]], 1)
    second = jnp.concatenate([odd[:BLOCK], got[1, :, :640]], 1)
    later = jnp.concatenate(
        [
            jnp.concatenate([even[BLOCK:], got[0, :, 640:]], 1),
            jnp.concatenate([odd[BLOCK:], got[1, :, 640:]], 1),
        ],
        0,
    )
    columns, scaled = panels(first, second, inverses, 512)
    picked = jnp.concatenate([scaled[:, :256], scaled[:, 640:]], 1)
    later = (later.astype(F32) - dot_tn(columns[:, 640:], picked)).astype(BF16)
    tile = (tile.astype(F32) - dot_tn(scaled[:, 256:512], columns[:, :256])).astype(BF16)
    return jnp.concatenate(
        [
            tile,
            tile[:, 128:160].T,
            lax.dynamic_slice_in_dim(later[:, 256:], 32 * s, 32, 0),
            lax.dynamic_slice_in_dim(later[:, :256], 32 * u, 32, 0),
        ],
        0,
    )


def local(leaf_fronts, pivot_entries, pivot_inverse, block_map_one, block_map_two, block_map_top):
    k, zl, xl, c = (lax.axis_index(name) for name in ("k", "zl", "xl", "c"))
    s = lax.axis_index("sub")
    u = zl * 4 + xl * 2 + c
    p = k * 8 + u
    maps = (block_map_one, block_map_two, block_map_top)
    payload = leaf_stage(
        leaf_fronts, lax.dynamic_index_in_dim(pivot_inverse, k, 0, keepdims=False), zl, xl, c, u, s
    )
    whole = gather_ring(payload, k, 8)
    tiles = whole[:, :256]
    got = lax.all_to_all(
        jnp.broadcast_to(whole[None, :, 256:320], (8, 8, 64, 256)), "sub", 0, 0, tiled=True
    )
    got = got.reshape(8, 8, 2, 32, 256)
    own = got[:, :, 0].reshape(8, 8, 2, 16, 256).transpose(1, 2, 0, 3, 4).reshape(8, 2, BLOCK, 256)
    core = got[:, :, 1].transpose(1, 0, 2, 3).reshape(8, 256, 256)
    mine = lax.all_to_all(
        jnp.broadcast_to(whole[None, :, 320:], (4, 8, 32, 256)), ("zl", "xl"), 0, 0, tiled=True
    )
    other = lax.ppermute(mine, "c", [(0, 1), (1, 0)])
    pair = jnp.stack([jnp.where(c == 0, mine, other), jnp.where(c == 0, other, mine)], 1)
    cols = pair.transpose(2, 0, 1, 3, 4).reshape(8, 256, 256)

    slots = {(3, 0): [p, p + 64]}
    for level in (2, 1, 0):
        for front in range(8 >> level):
            block_list = maps[level][front // 2, front % 2]
            slots[level, front] = [find(block_list, spot) for spot in slots[level + 1, front // 2]]

    rows, panel = [], []
    for front in range(8):
        row_parts, panel_parts = [], []
        for spot in slots[0, front]:
            row = jnp.where(spot >= 8, tiles[front, BLOCK:], tiles[front, :BLOCK])
            row_parts.append(jnp.where(spot >= 0, row, 0))
            part = jnp.where(spot >= 8, own[front, :, :, BLOCK:], own[front, :, :, :BLOCK])
            panel_parts.append(jnp.where(spot >= 0, part, 0))
        rows.append(jnp.concatenate(row_parts, 0))
        panel.append(jnp.concatenate(panel_parts, 2))
    core = [core[f].reshape(2, BLOCK, 256) for f in range(8)]
    cols = [cols[f].reshape(2, BLOCK, 256) for f in range(8)]

    for level in (1, 2, 3):
        half = 4 << level
        width = 256 << level
        wanted = 4 if level < 3 else 2
        new_rows, new_panel, new_core, new_cols = [], [], [], []
        for front in range(8 >> level):
            pivots = pivot_entries[8 - (16 >> level) + front]
            inverses = pivot_inverse[16 - (16 >> level) + front]
            pair_map = maps[level - 1][front]
            goal = (0, 1, 2 * half, 2 * half + 1)
            mask = [
                [(pair_map[child, half - 2 + q % 2] == goal[q]).astype(BF16) for q in range(4)]
                for child in range(2)
            ]
            place = jnp.concatenate(
                [placement(pair_map[child], 4 * half, 16) for child in range(2)], 0
            )
            kids = (2 * front, 2 * front + 1)
            lhs = [
                jnp.concatenate([cols[kid][q % 2] * mask[i][q] for i, kid in enumerate(kids)], 1)
                for q in range(wanted)
            ]
            lhs.append(jnp.concatenate([rows[kid] for kid in kids], 1))
            placed = dot(jnp.concatenate(lhs, 0), place)
            z = []
            for q in range(wanted):
                col_part = placed[q * BLOCK : (q + 1) * BLOCK]
                own_part = sum(panel[kid][q % 2].astype(F32) * mask[i][q] for i, kid in enumerate(kids))
                core_part = [
                    sum(
                        core[kid][q % 2, :, (r % 2) * BLOCK : (r % 2 + 1) * BLOCK].astype(F32)
                        * (mask[i][q] * mask[i][r])
                        for i, kid in enumerate(kids)
                    )
                    for r in ((2, 3, 1) if level < 3 else (1,))
                ]
                if q == 0:
                    core_part[-1] = core_part[-1] + pivots[:BLOCK, BLOCK:].astype(F32)
                if level == 3 and q < 2:
                    entries = pivots[q * BLOCK : (q + 1) * BLOCK].astype(F32)
                    mine = jnp.where(p == 0, entries[:, :BLOCK], entries[:, BLOCK:])
                    mine = jnp.where(p < 2, mine, 0)
                    own_part = own_part + jnp.pad(mine, ((0, 0), (0, BLOCK)))
                    part = lax.dynamic_index_in_dim(
                        entries.reshape(BLOCK, 2, 8, 16), s, 2, keepdims=False
                    ).reshape(BLOCK, 32)
                    col_part = col_part + jnp.pad(part, ((0, 0), (0, width - 32)))
                z.append(jnp.concatenate([col_part, own_part] + core_part, 1).astype(BF16))
            live = z[0].shape[1] - BLOCK
            columns, scaled = panels(z[0], z[1], inverses, live)
            row = placed[wanted * BLOCK :] - dot_tn(
                scaled[:, width : width + 256], columns[:, :width]
            )
            if level == 3:
                strip = lax.dynamic_index_in_dim(
                    pivots.reshape(256, 2, 8, 16), s, 2, keepdims=False
                ).reshape(256, 32)
                strip = jnp.where(p == 0, strip[:BLOCK], strip[BLOCK:]).astype(F32)
                strip = jnp.where(p < 2, strip, 0)
                row = row + jnp.pad(strip, ((0, BLOCK), (0, width - 32)))
                return row.astype(BF16)
            later = jnp.concatenate([z[2], z[3]], 0)[:, :live].astype(F32)
            later = later - dot_tn(columns[:, width + 256 : live], scaled[:, :live])
            later = later.astype(BF16).reshape(2, BLOCK, live)
            new_rows.append(row.astype(BF16))
            new_cols.append(later[:, :, :width])
            new_panel.append(later[:, :, width : width + 256])
            new_core.append(later[:, :, width + 256 :])
        rows, panel, core, cols = new_rows, new_panel, new_core, new_cols


def solution(mesh):
    cube = ("k", "zl", "xl", "c")
    split = Mesh(mesh.devices.reshape(8, 2, 2, 2, 8), cube + ("sub",))
    return jax.shard_map(
        local,
        mesh=split,
        in_specs=(P(cube, "sub"), P(), P(), P(), P(), P()),
        out_specs=P(cube, "sub"),
        check_vma=False,
    )
```

```python
import jax
import jax.numpy as jnp
from jax import lax
from jax.experimental import pallas as pl
from jax.experimental.pallas import tpu as pltpu
from jax.sharding import Mesh, PartitionSpec as P

BLOCK = 128
CHUNK = 256
F32 = jnp.float32
BF16 = jnp.bfloat16
MAP_START = (3, 3 + 112, 3 + 112 + 120)


def dot(lhs, rhs):
    return jnp.dot(lhs, rhs, preferred_element_type=F32)


def dot_tn(lhs, rhs):
    return lax.dot_general(lhs, rhs, (((0,), (0,)), ((), ())), preferred_element_type=F32)


def panels(first, second, inverse_zero, inverse_one, row_one):
    scaled_zero = dot(inverse_zero, first).astype(BF16)
    coupling = first[:, row_one : row_one + BLOCK]
    col_one = (second.astype(F32) - dot_tn(coupling, scaled_zero)).astype(BF16)
    scaled_one = dot(inverse_one, col_one).astype(BF16)
    columns = jnp.concatenate([first, col_one], 0)
    scaled = jnp.concatenate([scaled_zero, scaled_one], 0)
    return columns, scaled


def upper_kernel(
    info, whole, got, mine, other, pivots, inverses, out,
    z_one, z_two, z_top, y_one, y_two, y_top, t_one, t_two, own_one, own_two, core_one, core_two,
):
    p, s, c = info[0], info[1], info[2]
    z_refs = (None, z_one, z_two, z_top)
    y_refs = (None, y_one, y_two, y_top)
    t_refs = (None, t_one, t_two)
    own_refs = (None, own_one, own_two)
    core_refs = (None, core_one, core_two)

    def entry(level, front, child, index):
        count = (8 << level) - 2
        return info[MAP_START[level - 1] + (front * 2 + child) * count + index]

    def find(level, front, child, wanted):
        group = 4 << level
        low = lax.rem(p, group)
        first = entry(level, front, child, jnp.maximum(low - 2, 0))
        second = entry(level, front, child, low + group - 2)
        spot = jnp.where(second == wanted, low + group, -1)
        return jnp.where((low >= 2) & (first == wanted), low, spot)

    slots = {(3, 0): [p, p + 64]}
    for level in (3, 2, 1):
        for front in range(16 >> level):
            slots[level - 1, front] = [
                find(level, front // 2, front % 2, spot) for spot in slots[level, front // 2]
            ]

    def leaf_slots(front, wide):
        parts = []
        for spot in slots[0, front]:
            part = jnp.where(spot >= 8, wide[:, BLOCK:], wide[:, :BLOCK])
            parts.append(jnp.where(spot >= 0, part, jnp.zeros_like(part)))
        return jnp.concatenate(parts, 1)

    def leaf_own(front, q):
        stacked = [got[sub, front, 16 * q : 16 * q + 16, :] for sub in range(8)]
        return leaf_slots(front, jnp.concatenate(stacked, 0))

    def leaf_core(front):
        return jnp.concatenate([got[sub, front, 32:64, :] for sub in range(8)], 0)

    for level in (1, 2, 3):
        z_ref, y_ref = z_refs[level], y_refs[level]
        group = 4 << level
        width = 256 << level
        wanted = 4 if level < 3 else 2
        z_ref[...] = jnp.zeros_like(z_ref)
        y_ref[...] = jnp.zeros_like(y_ref)
        for front in range(8 >> level):
            kids = (2 * front, 2 * front + 1)
            goal = (0, 1, 2 * group, 2 * group + 1)
            mask = [
                [entry(level, front, child, group - 2 + q % 2) == goal[q] for q in range(4)]
                for child in range(2)
            ]

            def masked(child, q, value):
                return jnp.where(mask[child][q], value, jnp.zeros_like(value))

            for child, kid in enumerate(kids):
                def put(block, dest, panel, row):
                    spread = [
                        masked(child, q, panel[:, (q % 2) * BLOCK : (q % 2 + 1) * BLOCK])
                        for q in range(wanted)
                    ]
                    spread = jnp.concatenate(spread, 1)
                    at = pl.ds(pl.multiple_of(dest * 16, 16), 16)
                    if child == 1:
                        spread = spread + z_ref[front, at, :]
                        row = row + y_ref[front, at, :]
                    z_ref[front, at, :] = spread
                    y_ref[front, at, :] = row

                if level == 1:
                    for block in range(2, 16):
                        here = (block // 4, kid, pl.ds(16 * (block % 2), 16))
                        panel = jnp.where(c == block // 2 % 2, mine[here], other[here])
                        row = leaf_slots(kid, whole[kid, 16 * block : 16 * block + 16, :])
                        put(block, entry(level, front, child, block - 2), panel, row)
                else:
                    def step(block, carry):
                        at = pl.ds(pl.multiple_of(block * 16, 16), 16)
                        put(
                            block,
                            entry(level, front, child, block - 2),
                            t_refs[level - 1][kid, at, :],
                            y_refs[level - 1][kid, at, :],
                        )
                        return carry

                    lax.fori_loop(2, 2 * group, step, 0, unroll=6)

            if level == 3:
                lane_part = []
                for half in range(2):
                    at = pl.ds(pl.multiple_of(half * BLOCK + 16 * s, 16), 16)
                    strip = pivots[6, at, :]
                    z_ref[0, 16 * half : 16 * half + 16, :] += strip
                    strip = jnp.where(p == 0, strip[:, :BLOCK], strip[:, BLOCK:])
                    strip = jnp.where(p < 2, strip, jnp.zeros_like(strip))
                    y_ref[0, 16 * half : 16 * half + 16, :BLOCK] += strip

            core_rows = (2, 3, 1) if level < 3 else (1,)
            zt = []
            for q in range(wanted):
                parts = []
                own = jnp.zeros((BLOCK, 256), F32)
                for child, kid in enumerate(kids):
                    if level == 1:
                        value = leaf_own(kid, q % 2)
                    else:
                        value = own_refs[level - 1][kid, (q % 2) * BLOCK : (q % 2 + 1) * BLOCK, :]
                    own = own + masked(child, q, value.astype(F32))
                if level == 3:
                    strip = pivots[6, q * BLOCK : (q + 1) * BLOCK, :].astype(F32)
                    strip = jnp.where(p == 0, strip[:, :BLOCK], strip[:, BLOCK:])
                    strip = jnp.where(p < 2, strip, jnp.zeros_like(strip))
                    own = own + jnp.concatenate([strip, jnp.zeros_like(strip)], 1)
                parts.append(own)
                for r in core_rows:
                    value = jnp.zeros((BLOCK, BLOCK), F32)
                    for child, kid in enumerate(kids):
                        if level == 1:
                            part = leaf_core(kid)[(q % 2) * BLOCK : (q % 2 + 1) * BLOCK]
                        else:
                            part = core_refs[level - 1][kid, (q % 2) * BLOCK : (q % 2 + 1) * BLOCK, :]
                        part = part[:, (r % 2) * BLOCK : (r % 2 + 1) * BLOCK].astype(F32)
                        value = value + masked(child, q, masked(child, r, part))
                    if q == 0 and r == 1:
                        value = value + pivots[
                            8 - (16 >> level) + front, :BLOCK, BLOCK:
                        ].astype(F32)
                    parts.append(value)
                zt.append(jnp.concatenate(parts, 1).astype(BF16))
            live = zt[0].shape[1] - BLOCK
            inverse_zero = inverses[16 - (16 >> level) + front, 0]
            inverse_one = inverses[16 - (16 >> level) + front, 1]
            columns, scaled = panels(zt[0], zt[1], inverse_zero, inverse_one, live)
            coupling = columns[:BLOCK, live:]
            own_scaled = scaled[:, :256]
            if level < 3:
                core_cols = columns[:, 256:512]
                later = jnp.concatenate([zt[2], zt[3]], 0)[:, :512].astype(F32)
                later = (later - dot_tn(core_cols, scaled[:, :512])).astype(BF16)
                own_refs[level][front] = later[:, :256]
                core_refs[level][front] = later[:, 256:]
            for start in range(0, width, CHUNK):
                at = pl.ds(start, CHUNK)
                first = z_ref[front, at, :BLOCK]
                scaled_zero = dot(first, inverse_zero).astype(BF16)
                second = z_ref[front, at, BLOCK : 2 * BLOCK].astype(F32)
                second = (second - dot(scaled_zero, coupling)).astype(BF16)
                row = y_ref[front, at, :].astype(F32)
                row = row - dot(jnp.concatenate([first, second], 1), own_scaled)
                if level == 3:
                    out[:, start : start + CHUNK] = row.T.astype(BF16)
                    continue
                y_ref[front, at, :] = row.astype(BF16)
                scaled_one = dot(second, inverse_one).astype(BF16)
                rest = z_ref[front, at, 2 * BLOCK :].astype(F32)
                rest = rest - dot(jnp.concatenate([scaled_zero, scaled_one], 1), core_cols)
                t_refs[level][front, at, :] = rest.astype(BF16)


def upper_levels(info, whole, got, mine, other, pivots, inverses):
    vmem = pl.BlockSpec(memory_space=pltpu.VMEM)
    return pl.pallas_call(
        upper_kernel,
        out_shape=jax.ShapeDtypeStruct((256, 2048), BF16),
        in_specs=[pl.BlockSpec(memory_space=pltpu.SMEM)] + [vmem] * 6,
        out_specs=vmem,
        scratch_shapes=[
            pltpu.VMEM(shape, BF16)
            for shape in (
                (4, 512, 512), (2, 1024, 512), (1, 2048, 256),
                (4, 512, 256), (2, 1024, 256), (1, 2048, 256),
                (4, 512, 256), (2, 1024, 256),
                (4, 256, 256), (2, 256, 256), (4, 256, 256), (2, 256, 256),
            )
        ],
        compiler_params=pltpu.CompilerParams(vmem_limit_bytes=48 * 2**20),
        name="upper_levels",
    )(info, whole, got, mine, other, pivots, inverses)


def gather_ring(payload, k, count):
    parts = [(payload, k)]
    ahead = behind = payload
    up = [(i, (i + 1) % count) for i in range(count)]
    down = [(i, (i - 1) % count) for i in range(count)]
    for step in range(1, count // 2 + 1):
        ahead = lax.ppermute(ahead, "k", up)
        parts.append((ahead, (k - step) % count))
        if step < count // 2:
            behind = lax.ppermute(behind, "k", down)
            parts.append((behind, (k + step) % count))
    whole = jnp.zeros((count,) + payload.shape, payload.dtype)
    for part, spot in parts:
        whole = lax.dynamic_update_slice_in_dim(whole, part[None], spot, 0)
    return whole


def leaf_stage(leaf, inverses, zl, xl, c, u, s):
    tile = leaf
    spread = jnp.where(xl == 0, tile, lax.ppermute(tile, "xl", [(0, 1)]))
    spread = jnp.where(zl == 0, spread, lax.ppermute(spread, "zl", [(0, 1)]))
    other = lax.ppermute(spread, "c", [(0, 1), (1, 0)])
    even = jnp.where(c == 0, spread, other)
    odd = jnp.where(c == 0, other, spread)
    piece = jnp.concatenate(
        [
            tile[:, :32],
            odd[:BLOCK, :32],
            even[BLOCK:, :32],
            odd[BLOCK:, :32],
            even[BLOCK:, 128:160],
            odd[BLOCK:, 128:160],
        ],
        0,
    ).T
    got = lax.all_to_all(jnp.broadcast_to(piece[None], (8,) + piece.shape), "sub", 0, 0, tiled=True)
    got = got.reshape(8, 2, 16, 896).transpose(1, 0, 2, 3).reshape(2, BLOCK, 896)
    first = jnp.concatenate([even[:BLOCK], got[0, :, :640]], 1)
    second = jnp.concatenate([odd[:BLOCK], got[1, :, :640]], 1)
    columns, scaled = panels(first, second, inverses[0], inverses[1], 512)
    core = got[:, :, 640:].reshape(256, 256).astype(F32)
    core = core - dot_tn(columns[:, 640:], scaled[:, 640:])
    cols = jnp.concatenate([even[BLOCK:], odd[BLOCK:]], 0).T.astype(F32)
    cols = cols - dot_tn(scaled[:, :256], columns[:, 640:])
    tile = tile.T.astype(F32) - dot_tn(columns[:, :256], scaled[:, 256:512])
    return jnp.concatenate(
        [
            tile.astype(BF16),
            lax.dynamic_slice_in_dim(core.astype(BF16), 32 * s, 32, 0),
            lax.dynamic_slice_in_dim(cols.astype(BF16), 32 * u, 32, 0),
        ],
        0,
    )


def local(leaf_fronts, pivot_entries, pivot_inverse, block_map_one, block_map_two, block_map_top):
    k, zl, xl, c = (lax.axis_index(name) for name in ("k", "zl", "xl", "c"))
    s = lax.axis_index("sub")
    u = zl * 4 + xl * 2 + c
    maps = (block_map_one, block_map_two, block_map_top)
    info = jnp.concatenate(
        [jnp.stack([k * 8 + u, s, c]).astype(jnp.int32)] + [table.reshape(-1) for table in maps]
    )
    payload = leaf_stage(
        leaf_fronts, lax.dynamic_index_in_dim(pivot_inverse, k, 0, keepdims=False), zl, xl, c, u, s
    )
    whole = gather_ring(payload, k, 8)
    mine = lax.all_to_all(
        jnp.broadcast_to(whole[None, :, 288:], (4, 8, 32, 256)), ("zl", "xl"), 0, 0, tiled=True
    )
    other = lax.ppermute(mine, "c", [(0, 1), (1, 0)])
    piece = jnp.concatenate([whole[:, 128:160], whole[:, 256:288]], 1)
    got = lax.all_to_all(jnp.broadcast_to(piece[None], (8, 8, 64, 256)), "sub", 0, 0, tiled=True)
    return upper_levels(info, whole, got, mine, other, pivot_entries, pivot_inverse)


def solution(mesh):
    cube = ("k", "zl", "xl", "c")
    split = Mesh(mesh.devices.reshape(8, 2, 2, 2, 8), cube + ("sub",))
    return jax.shard_map(
        local,
        mesh=split,
        in_specs=(P(cube, "sub"), P(), P(), P(), P(), P()),
        out_specs=P(cube, "sub"),
        check_vma=False,
    )
```

```python
import jax
import jax.numpy as jnp
from jax import lax
from jax.experimental import pallas as pl
from jax.experimental.pallas import tpu as pltpu
from jax.sharding import Mesh, PartitionSpec as P

BLOCK = 128
CHUNK = 256
F32 = jnp.float32
BF16 = jnp.bfloat16
MAP_START = (3, 3 + 112, 3 + 112 + 120)


def dot(lhs, rhs):
    return jnp.dot(lhs, rhs, preferred_element_type=F32)


def dot_tn(lhs, rhs):
    return lax.dot_general(lhs, rhs, (((0,), (0,)), ((), ())), preferred_element_type=F32)


def panels(first, second, inverse_zero, inverse_one, row_one):
    scaled_zero = dot(inverse_zero, first).astype(BF16)
    coupling = first[:, row_one : row_one + BLOCK]
    col_one = (second.astype(F32) - dot_tn(coupling, scaled_zero)).astype(BF16)
    scaled_one = dot(inverse_one, col_one).astype(BF16)
    columns = jnp.concatenate([first, col_one], 0)
    scaled = jnp.concatenate([scaled_zero, scaled_one], 0)
    return columns, scaled


def upper_kernel(
    info, whole, got, near, other, pivots, inverses, out,
    z_one, z_two, z_top, y_one, y_two, y_top, t_one, t_two, own_one, own_two, core_one, core_two,
):
    p, s, c = info[0], info[1], info[2]
    z_refs = (None, z_one, z_two, z_top)
    y_refs = (None, y_one, y_two, y_top)
    t_refs = (None, t_one, t_two)
    own_refs = (None, own_one, own_two)
    core_refs = (None, core_one, core_two)

    def entry(level, front, child, index):
        count = (8 << level) - 2
        return info[MAP_START[level - 1] + (front * 2 + child) * count + index]

    def find(level, front, child, wanted):
        group = 4 << level
        low = lax.rem(p, group)
        first = entry(level, front, child, jnp.maximum(low - 2, 0))
        second = entry(level, front, child, low + group - 2)
        spot = jnp.where(second == wanted, low + group, -1)
        return jnp.where((low >= 2) & (first == wanted), low, spot)

    slots = {(3, 0): [p, p + 64]}
    for level in (3, 2, 1):
        for front in range(16 >> level):
            slots[level - 1, front] = [
                find(level, front // 2, front % 2, spot) for spot in slots[level, front // 2]
            ]

    def leaf_slots(front, wide):
        parts = []
        for spot in slots[0, front]:
            part = jnp.where(spot >= 8, wide[:, BLOCK:], wide[:, :BLOCK])
            parts.append(jnp.where(spot >= 0, part, jnp.zeros_like(part)))
        return jnp.concatenate(parts, 1)

    def stacked(front, lanes):
        return jnp.concatenate([got[sub, front, :, lanes] for sub in range(8)], 0)

    def leaf_own(front, q):
        return leaf_slots(front, stacked(front, slice(256 * q, 256 * q + 256)))

    def leaf_core(front):
        blocks = stacked(front, slice(512, 896))
        turned = blocks[:, BLOCK : 2 * BLOCK].astype(F32).T.astype(BF16)
        return blocks[:, : 2 * BLOCK], jnp.concatenate([turned, blocks[:, 2 * BLOCK :]], 1)

    for level in (1, 2, 3):
        z_ref, y_ref = z_refs[level], y_refs[level]
        group = 4 << level
        width = 256 << level
        wanted = 4 if level < 3 else 2
        z_ref[...] = jnp.zeros_like(z_ref)
        y_ref[...] = jnp.zeros_like(y_ref)
        for front in range(8 >> level):
            kids = (2 * front, 2 * front + 1)
            goal = (0, 1, 2 * group, 2 * group + 1)
            mask = [
                [entry(level, front, child, group - 2 + q % 2) == goal[q] for q in range(4)]
                for child in range(2)
            ]

            def masked(child, q, value):
                return jnp.where(mask[child][q], value, jnp.zeros_like(value))

            for child, kid in enumerate(kids):
                def put(block, dest, panel, row):
                    spread = [
                        masked(child, q, panel[:, (q % 2) * BLOCK : (q % 2 + 1) * BLOCK])
                        for q in range(wanted)
                    ]
                    spread = jnp.concatenate(spread, 1)
                    at = pl.ds(pl.multiple_of(dest * 16, 16), 16)
                    if child == 1:
                        spread = spread + z_ref[front, at, :]
                        row = row + y_ref[front, at, :]
                    z_ref[front, at, :] = spread
                    y_ref[front, at, :] = row

                if level == 1:
                    for block in range(2, 16):
                        at = slice(16 * (block - 2), 16 * (block - 1))
                        one, two = near[kid, at, :], other[kid, at, :]
                        panel = jnp.concatenate(
                            [jnp.where(c == 0, one, two), jnp.where(c == 0, two, one)], 1
                        )
                        row = leaf_slots(kid, whole[kid, at, :])
                        put(block, entry(level, front, child, block - 2), panel, row)
                else:
                    def step(block, carry):
                        at = pl.ds(pl.multiple_of(block * 16, 16), 16)
                        put(
                            block,
                            entry(level, front, child, block - 2),
                            t_refs[level - 1][kid, at, :],
                            y_refs[level - 1][kid, at, :],
                        )
                        return carry

                    lax.fori_loop(2, 2 * group, step, 0, unroll=6)

            if level == 3:
                lane_part = []
                for half in range(2):
                    at = pl.ds(pl.multiple_of(half * BLOCK + 16 * s, 16), 16)
                    strip = pivots[6, at, :]
                    z_ref[0, 16 * half : 16 * half + 16, :] += strip
                    strip = jnp.where(p == 0, strip[:, :BLOCK], strip[:, BLOCK:])
                    strip = jnp.where(p < 2, strip, jnp.zeros_like(strip))
                    y_ref[0, 16 * half : 16 * half + 16, :BLOCK] += strip

            core_rows = (2, 3, 1) if level < 3 else (1,)
            if level == 1:
                kid_own = [[leaf_own(kid, q) for q in range(2)] for kid in kids]
                kid_core = [leaf_core(kid) for kid in kids]
            zt = []
            for q in range(wanted):
                parts = []
                own = jnp.zeros((BLOCK, 256), F32)
                for child, kid in enumerate(kids):
                    if level == 1:
                        value = kid_own[child][q % 2]
                    else:
                        value = own_refs[level - 1][kid, (q % 2) * BLOCK : (q % 2 + 1) * BLOCK, :]
                    own = own + masked(child, q, value.astype(F32))
                if level == 3:
                    strip = pivots[6, q * BLOCK : (q + 1) * BLOCK, :].astype(F32)
                    strip = jnp.where(p == 0, strip[:, :BLOCK], strip[:, BLOCK:])
                    strip = jnp.where(p < 2, strip, jnp.zeros_like(strip))
                    own = own + jnp.concatenate([strip, jnp.zeros_like(strip)], 1)
                parts.append(own)
                for r in core_rows:
                    value = jnp.zeros((BLOCK, BLOCK), F32)
                    for child, kid in enumerate(kids):
                        if level == 1:
                            part = kid_core[child][q % 2]
                        else:
                            part = core_refs[level - 1][kid, (q % 2) * BLOCK : (q % 2 + 1) * BLOCK, :]
                        part = part[:, (r % 2) * BLOCK : (r % 2 + 1) * BLOCK].astype(F32)
                        value = value + masked(child, q, masked(child, r, part))
                    if q == 0 and r == 1:
                        value = value + pivots[
                            8 - (16 >> level) + front, :BLOCK, BLOCK:
                        ].astype(F32)
                    parts.append(value)
                zt.append(jnp.concatenate(parts, 1).astype(BF16))
            live = zt[0].shape[1] - BLOCK
            inverse_zero = inverses[16 - (16 >> level) + front, 0]
            inverse_one = inverses[16 - (16 >> level) + front, 1]
            columns, scaled = panels(zt[0], zt[1], inverse_zero, inverse_one, live)
            coupling = columns[:BLOCK, live:]
            own_scaled = scaled[:, :256]
            if level < 3:
                core_cols = columns[:, 256:512]
                later = jnp.concatenate([zt[2], zt[3]], 0)[:, :512].astype(F32)
                later = (later - dot_tn(core_cols, scaled[:, :512])).astype(BF16)
                own_refs[level][front] = later[:, :256]
                core_refs[level][front] = later[:, 256:]
            for start in range(0, width, CHUNK):
                at = pl.ds(start, CHUNK)
                first = z_ref[front, at, :BLOCK]
                scaled_zero = dot(first, inverse_zero).astype(BF16)
                second = z_ref[front, at, BLOCK : 2 * BLOCK].astype(F32)
                second = (second - dot(scaled_zero, coupling)).astype(BF16)
                row = y_ref[front, at, :].astype(F32)
                row = row - dot(jnp.concatenate([first, second], 1), own_scaled)
                if level == 3:
                    out[:, start : start + CHUNK] = row.T.astype(BF16)
                    continue
                y_ref[front, at, :] = row.astype(BF16)
                scaled_one = dot(second, inverse_one).astype(BF16)
                rest = z_ref[front, at, 2 * BLOCK :].astype(F32)
                rest = rest - dot(jnp.concatenate([scaled_zero, scaled_one], 1), core_cols)
                t_refs[level][front, at, :] = rest.astype(BF16)


def upper_levels(info, whole, got, near, other, pivots, inverses):
    vmem = pl.BlockSpec(memory_space=pltpu.VMEM)
    return pl.pallas_call(
        upper_kernel,
        out_shape=jax.ShapeDtypeStruct((256, 2048), BF16),
        in_specs=[pl.BlockSpec(memory_space=pltpu.SMEM)] + [vmem] * 6,
        out_specs=vmem,
        scratch_shapes=[
            pltpu.VMEM(shape, BF16)
            for shape in (
                (4, 512, 512), (2, 1024, 512), (1, 2048, 256),
                (4, 512, 256), (2, 1024, 256), (1, 2048, 256),
                (4, 512, 256), (2, 1024, 256),
                (4, 256, 256), (2, 256, 256), (4, 256, 256), (2, 256, 256),
            )
        ],
        compiler_params=pltpu.CompilerParams(vmem_limit_bytes=48 * 2**20),
        name="upper_levels",
    )(info, whole, got, near, other, pivots, inverses)


def leaf_stage(leaf, inverses, zl, xl, c, s):
    tile = leaf
    spread = jnp.where(xl == 0, tile, lax.ppermute(tile, "xl", [(0, 1)]))
    spread = jnp.where(zl == 0, spread, lax.ppermute(spread, "zl", [(0, 1)]))
    other = lax.ppermute(spread, "c", [(0, 1), (1, 0)])
    even = jnp.where(c == 0, spread, other)
    odd = jnp.where(c == 0, other, spread)
    piece = jnp.concatenate(
        [
            tile[:, :32],
            odd[:BLOCK, :32],
            even[BLOCK:, :32],
            odd[BLOCK:, :32],
            even[BLOCK:, 128:160],
            odd[BLOCK:, 128:160],
        ],
        0,
    ).T
    got = lax.all_to_all(jnp.broadcast_to(piece[None], (8,) + piece.shape), "sub", 0, 0, tiled=True)
    got = got.reshape(8, 2, 16, 896).transpose(1, 0, 2, 3).reshape(2, BLOCK, 896)
    first = jnp.concatenate([even[:BLOCK], got[0, :, :640]], 1)
    second = jnp.concatenate([odd[:BLOCK], got[1, :, :640]], 1)
    columns, scaled = panels(first, second, inverses[0], inverses[1], 512)
    core = got[:, :, 640:].reshape(256, 256).astype(F32)
    core = core - dot_tn(columns[:, 640:], scaled[:, 640:])
    core = core.astype(BF16)
    core = jnp.concatenate([core[:BLOCK, :BLOCK], core[:BLOCK, BLOCK:], core[BLOCK:, BLOCK:]], 1)
    core = lax.dynamic_slice_in_dim(core, 16 * s, 16, 0)
    tile = tile.T.astype(F32) - dot_tn(columns[:, :256], scaled[:, 256:512])
    rest = jnp.concatenate([core[:8, 256:], core[8:, 256:]], 1)
    return jnp.concatenate([tile[32:].astype(BF16), core[:, :256], rest], 0)


def local(leaf_fronts, pivot_entries, pivot_inverse, block_map_one, block_map_two, block_map_top):
    k, zl, xl, c = (lax.axis_index(name) for name in ("k", "zl", "xl", "c"))
    s = lax.axis_index("sub")
    u = zl * 4 + xl * 2 + c
    maps = (block_map_one, block_map_two, block_map_top)
    info = jnp.concatenate(
        [jnp.stack([k * 8 + u, s, c]).astype(jnp.int32)] + [table.reshape(-1) for table in maps]
    )
    payload = leaf_stage(
        leaf_fronts, lax.dynamic_index_in_dim(pivot_inverse, k, 0, keepdims=False), zl, xl, c, s
    )
    whole = lax.all_gather(payload, "k")
    rest = jnp.concatenate([whole[:, 240:, :BLOCK], whole[:, 240:, BLOCK:]], 1)
    piece = jnp.concatenate([whole[:, 96:112], whole[:, 112:128], whole[:, 224:240], rest], 2)
    got = lax.all_to_all(jnp.broadcast_to(piece[None], (8, 8, 16, 896)), "sub", 0, 0, tiled=True)

    def spread(value, axis, position):
        return jnp.where(position == 0, value, lax.ppermute(value, axis, [(0, 1)]))

    later = whole[:, :224, BLOCK:]
    near = jnp.concatenate(
        [
            spread(spread(later[:4], "xl", xl), "zl", zl),
            spread(spread(later[4:], "zl", zl), "xl", xl),
        ],
        0,
    )
    other = lax.ppermute(near, "c", [(0, 1), (1, 0)])
    return upper_levels(info, whole, got, near, other, pivot_entries, pivot_inverse)


def solution(mesh):
    cube = ("k", "zl", "xl", "c")
    split = Mesh(mesh.devices.reshape(8, 2, 2, 2, 8), cube + ("sub",))
    return jax.shard_map(
        local,
        mesh=split,
        in_specs=(P(cube, "sub"), P(), P(), P(), P(), P()),
        out_specs=P(cube, "sub"),
        check_vma=False,
    )
```

```python
import jax
import jax.numpy as jnp
from jax import lax
from jax.experimental import pallas as pl
from jax.experimental.pallas import tpu as pltpu
from jax.sharding import Mesh, PartitionSpec as P

BLOCK = 128
CHUNK = 256
F32 = jnp.float32
BF16 = jnp.bfloat16
CORE_AT = 8 * 224
MAP_START = (3, 3 + 112, 3 + 112 + 120)


def dot(lhs, rhs):
    return jnp.dot(lhs, rhs, preferred_element_type=F32)


def dot_tn(lhs, rhs):
    return lax.dot_general(lhs, rhs, (((0,), (0,)), ((), ())), preferred_element_type=F32)


def panels(first, second, inverse_zero, inverse_one, row_one):
    scaled_zero = dot(inverse_zero, first).astype(BF16)
    coupling = first[:, row_one : row_one + BLOCK]
    col_one = (second.astype(F32) - dot_tn(coupling, scaled_zero)).astype(BF16)
    scaled_one = dot(inverse_one, col_one).astype(BF16)
    columns = jnp.concatenate([first, col_one], 0)
    scaled = jnp.concatenate([scaled_zero, scaled_one], 0)
    return columns, scaled


def upper_kernel(
    info, whole, got, near, other, pivots, all_inverses, out,
    z_one, z_two, z_top, y_one, y_two, y_top, t_one, t_two, own_one, own_two, core_one, core_two,
    couplings, top, inverses, arrived,
):
    p, s, u = info[0], info[1], info[2]
    c = u % 2
    copies = [
        pltpu.make_async_copy(all_inverses.at[8:15], inverses, arrived.at[0]),
        pltpu.make_async_copy(pivots.at[0:7, 0:BLOCK, BLOCK : 2 * BLOCK], couplings, arrived.at[1]),
        pltpu.make_async_copy(pivots.at[6], top, arrived.at[2]),
    ]
    for copy in copies:
        copy.start()
    z_refs = (None, z_one, z_two, z_top)
    y_refs = (None, y_one, y_two, y_top)
    t_refs = (None, t_one, t_two)
    own_refs = (None, own_one, own_two)
    core_refs = (None, core_one, core_two)

    def entry(level, front, child, index):
        count = (8 << level) - 2
        return info[MAP_START[level - 1] + (front * 2 + child) * count + index]

    def find(level, front, child, wanted):
        group = 4 << level
        low = lax.rem(p, group)
        first = entry(level, front, child, jnp.maximum(low - 2, 0))
        second = entry(level, front, child, low + group - 2)
        spot = jnp.where(second == wanted, low + group, -1)
        return jnp.where((low >= 2) & (first == wanted), low, spot)

    slots = {(3, 0): [p, p + 64]}
    for level in (3, 2, 1):
        for front in range(16 >> level):
            slots[level - 1, front] = [
                find(level, front // 2, front % 2, spot) for spot in slots[level, front // 2]
            ]

    def leaf_slots(front, wide):
        parts = []
        for spot in slots[0, front]:
            part = jnp.where(spot >= 8, wide[:, BLOCK:], wide[:, :BLOCK])
            parts.append(jnp.where(spot >= 0, part, jnp.zeros_like(part)))
        return jnp.concatenate(parts, 1)

    def stacked(front, lanes):
        return jnp.concatenate([got[sub, front, :, lanes] for sub in range(8)], 0)

    def leaf_own(front, q):
        return leaf_slots(front, stacked(front, slice(256 * q, 256 * q + 256)))

    def share(other_u, front, part):
        apart = u ^ other_u
        start = CORE_AT + apart // 2 * 384 + front * 48 + part * 16
        at = pl.ds(pl.multiple_of(start, 16), 16)
        return jnp.where(apart % 2 == 0, near[at, :], other[at, :])

    def leaf_core(front):
        blocks = [
            jnp.concatenate([share(member, front, part) for member in range(8)], 0)
            for part in range(3)
        ]
        turned = blocks[1].astype(F32).T.astype(BF16)
        return jnp.concatenate(blocks[:2], 1), jnp.concatenate([turned, blocks[2]], 1)

    for level in (1, 2, 3):
        z_ref, y_ref = z_refs[level], y_refs[level]
        group = 4 << level
        width = 256 << level
        wanted = 4 if level < 3 else 2
        z_ref[...] = jnp.zeros_like(z_ref)
        y_ref[...] = jnp.zeros_like(y_ref)
        panels_t = []
        for front in range(8 >> level):
            kids = (2 * front, 2 * front + 1)
            goal = (0, 1, 2 * group, 2 * group + 1)
            mask = [
                [entry(level, front, child, group - 2 + q % 2) == goal[q] for q in range(4)]
                for child in range(2)
            ]

            def masked(child, q, value):
                return jnp.where(mask[child][q], value, jnp.zeros_like(value))

            for child, kid in enumerate(kids):
                def put(block, dest, panel, row):
                    spread = [
                        masked(child, q, panel[:, (q % 2) * BLOCK : (q % 2 + 1) * BLOCK])
                        for q in range(wanted)
                    ]
                    spread = jnp.concatenate(spread, 1)
                    at = pl.ds(pl.multiple_of(dest * 16, 16), 16)
                    if child == 1:
                        spread = spread + z_ref[front, at, :]
                        row = row + y_ref[front, at, :]
                    z_ref[front, at, :] = spread
                    y_ref[front, at, :] = row

                if level == 1:
                    for block in range(2, 16):
                        at = slice(16 * (block - 2), 16 * (block - 1))
                        start = kid * 224 + 16 * (block - 2)
                        one, two = near[start : start + 16, :], other[start : start + 16, :]
                        panel = jnp.concatenate(
                            [jnp.where(c == 0, one, two), jnp.where(c == 0, two, one)], 1
                        )
                        row = leaf_slots(kid, whole[kid, at, :])
                        put(block, entry(level, front, child, block - 2), panel, row)
                else:
                    def step(block, carry):
                        at = pl.ds(pl.multiple_of(block * 16, 16), 16)
                        put(
                            block,
                            entry(level, front, child, block - 2),
                            t_refs[level - 1][kid, at, :],
                            y_refs[level - 1][kid, at, :],
                        )
                        return carry

                    lax.fori_loop(2, 2 * group, step, 0, unroll=6)

            if level == 3:
                for half in range(2):
                    at = pl.ds(pl.multiple_of(half * BLOCK + 16 * s, 16), 16)
                    strip = top[at, :]
                    z_ref[0, 16 * half : 16 * half + 16, :] += strip
                    strip = jnp.where(p == 0, strip[:, :BLOCK], strip[:, BLOCK:])
                    strip = jnp.where(p < 2, strip, jnp.zeros_like(strip))
                    y_ref[0, 16 * half : 16 * half + 16, :BLOCK] += strip

            core_rows = (2, 3, 1) if level < 3 else (1,)
            if level == 1 and front == 0:
                for copy in copies:
                    copy.wait()
            if level == 1:
                kid_own = [[leaf_own(kid, q) for q in range(2)] for kid in kids]
                kid_core = [leaf_core(kid) for kid in kids]
            zt = []
            for q in range(wanted):
                parts = []
                own = jnp.zeros((BLOCK, 256), F32)
                for child, kid in enumerate(kids):
                    if level == 1:
                        value = kid_own[child][q % 2]
                    else:
                        value = own_refs[level - 1][kid, (q % 2) * BLOCK : (q % 2 + 1) * BLOCK, :]
                    own = own + masked(child, q, value.astype(F32))
                if level == 3:
                    strip = top[q * BLOCK : (q + 1) * BLOCK, :].astype(F32)
                    strip = jnp.where(p == 0, strip[:, :BLOCK], strip[:, BLOCK:])
                    strip = jnp.where(p < 2, strip, jnp.zeros_like(strip))
                    own = own + jnp.concatenate([strip, jnp.zeros_like(strip)], 1)
                parts.append(own)
                for r in core_rows:
                    value = jnp.zeros((BLOCK, BLOCK), F32)
                    for child, kid in enumerate(kids):
                        if level == 1:
                            part = kid_core[child][q % 2]
                        else:
                            part = core_refs[level - 1][kid, (q % 2) * BLOCK : (q % 2 + 1) * BLOCK, :]
                        part = part[:, (r % 2) * BLOCK : (r % 2 + 1) * BLOCK].astype(F32)
                        value = value + masked(child, q, masked(child, r, part))
                    if q == 0 and r == 1:
                        value = value + couplings[8 - (16 >> level) + front].astype(F32)
                    parts.append(value)
                zt.append(jnp.concatenate(parts, 1).astype(BF16))
            panels_t.append(zt)

        fronts = range(8 >> level)
        pieces = [(front, start) for front in fronts for start in range(0, width, CHUNK)]
        live = panels_t[0][0].shape[1] - BLOCK
        inverse = [
            [inverses[8 - (16 >> level) + front, q] for q in range(2)] for front in fronts
        ]

        def rows_of(ref, front, start, q):
            return ref[front, pl.ds(start, CHUNK), q * BLOCK : (q + 1) * BLOCK]

        scaled_zero_t = [dot(inverse[f][0], panels_t[f][0]).astype(BF16) for f in fronts]
        scaled_zero = [dot(rows_of(z_ref, f, at, 0), inverse[f][0]).astype(BF16) for f, at in pieces]
        second_t, second = [], []
        for f in fronts:
            coupling = panels_t[f][0][:, live:]
            value = panels_t[f][1].astype(F32) - dot_tn(coupling, scaled_zero_t[f])
            second_t.append(value.astype(BF16))
        for i, (f, at) in enumerate(pieces):
            coupling = panels_t[f][0][:, live:]
            value = rows_of(z_ref, f, at, 1).astype(F32) - dot(scaled_zero[i], coupling)
            second.append(value.astype(BF16))
        scaled_one_t = [dot(inverse[f][1], second_t[f]).astype(BF16) for f in fronts]
        if level < 3:
            scaled_one = [dot(second[i], inverse[f][1]).astype(BF16) for i, (f, _) in enumerate(pieces)]
            core_cols = [
                jnp.concatenate([panels_t[f][0][:, 256:512], second_t[f][:, 256:512]], 0)
                for f in fronts
            ]
            for f in fronts:
                later = jnp.concatenate([panels_t[f][2], panels_t[f][3]], 0)[:, :512].astype(F32)
                scaled = jnp.concatenate([scaled_zero_t[f][:, :512], scaled_one_t[f][:, :512]], 0)
                later = (later - dot_tn(core_cols[f], scaled)).astype(BF16)
                own_refs[level][f] = later[:, :256]
                core_refs[level][f] = later[:, 256:]
        for i, (f, at) in enumerate(pieces):
            own_scaled = jnp.concatenate([scaled_zero_t[f][:, :256], scaled_one_t[f][:, :256]], 0)
            columns = jnp.concatenate([rows_of(z_ref, f, at, 0), second[i]], 1)
            row = y_ref[f, pl.ds(at, CHUNK), :].astype(F32) - dot(columns, own_scaled)
            if level == 3:
                out[:, at : at + CHUNK] = row.T.astype(BF16)
                continue
            y_ref[f, pl.ds(at, CHUNK), :] = row.astype(BF16)
            rest = z_ref[f, pl.ds(at, CHUNK), 2 * BLOCK :].astype(F32)
            rest = rest - dot(jnp.concatenate([scaled_zero[i], scaled_one[i]], 1), core_cols[f])
            t_refs[level][f, pl.ds(at, CHUNK), :] = rest.astype(BF16)


def upper_levels(info, whole, got, near, other, pivots, inverses):
    vmem = pl.BlockSpec(memory_space=pltpu.VMEM)
    anywhere = pl.BlockSpec(memory_space=pltpu.HBM)
    return pl.pallas_call(
        upper_kernel,
        out_shape=jax.ShapeDtypeStruct((256, 2048), BF16),
        in_specs=[pl.BlockSpec(memory_space=pltpu.SMEM)] + [vmem] * 4 + [anywhere] * 2,
        out_specs=vmem,
        scratch_shapes=[
            pltpu.VMEM(shape, BF16)
            for shape in (
                (4, 512, 512), (2, 1024, 512), (1, 2048, 256),
                (4, 512, 256), (2, 1024, 256), (1, 2048, 256),
                (4, 512, 256), (2, 1024, 256),
                (4, 256, 256), (2, 256, 256), (4, 256, 256), (2, 256, 256),
                (7, BLOCK, BLOCK), (256, 256), (7, 2, BLOCK, BLOCK),
            )
        ]
        + [pltpu.SemaphoreType.DMA((3,))],
        compiler_params=pltpu.CompilerParams(vmem_limit_bytes=62 * 2**20),
        name="upper_levels",
    )(info, whole, got, near, other, pivots, inverses)


def leaf_stage(leaf, inverses, zl, xl, c, u):
    tile = leaf
    spread = jnp.where(xl == 0, tile, lax.ppermute(tile, "xl", [(0, 1)]))
    spread = jnp.where(zl == 0, spread, lax.ppermute(spread, "zl", [(0, 1)]))
    other = lax.ppermute(spread, "c", [(0, 1), (1, 0)])
    even = jnp.where(c == 0, spread, other)
    odd = jnp.where(c == 0, other, spread)
    piece = jnp.concatenate(
        [
            tile[:, :32],
            odd[:BLOCK, :32],
            even[BLOCK:, :32],
            odd[BLOCK:, :32],
            even[BLOCK:, 128:160],
            odd[BLOCK:, 128:160],
        ],
        0,
    ).T
    got = lax.all_to_all(jnp.broadcast_to(piece[None], (8,) + piece.shape), "sub", 0, 0, tiled=True)
    got = got.reshape(8, 2, 16, 896).transpose(1, 0, 2, 3).reshape(2, BLOCK, 896)
    first = jnp.concatenate([even[:BLOCK], got[0, :, :640]], 1)
    second = jnp.concatenate([odd[:BLOCK], got[1, :, :640]], 1)
    columns, scaled = panels(first, second, inverses[0], inverses[1], 512)
    core = got[:, :, 640:].reshape(256, 256).astype(F32)
    core = core - dot_tn(columns[:, 640:], scaled[:, 640:])
    core = core.astype(BF16)
    core = jnp.concatenate([core[:BLOCK, :BLOCK], core[:BLOCK, BLOCK:], core[BLOCK:, BLOCK:]], 1)
    core = lax.dynamic_slice_in_dim(core, 16 * u, 16, 0)
    tile = tile.T.astype(F32) - dot_tn(columns[:, :256], scaled[:, 256:512])
    rest = jnp.concatenate([core[:8, 256:], core[8:, 256:]], 1)
    return jnp.concatenate([tile[32:].astype(BF16), core[:, :256], rest], 0)


def local(leaf_fronts, pivot_entries, pivot_inverse, block_map_one, block_map_two, block_map_top):
    k, zl, xl, c = (lax.axis_index(name) for name in ("k", "zl", "xl", "c"))
    s = lax.axis_index("sub")
    u = zl * 4 + xl * 2 + c
    maps = (block_map_one, block_map_two, block_map_top)
    info = jnp.concatenate(
        [jnp.stack([k * 8 + u, s, u]).astype(jnp.int32)] + [table.reshape(-1) for table in maps]
    )
    payload = leaf_stage(
        leaf_fronts, lax.dynamic_index_in_dim(pivot_inverse, k, 0, keepdims=False), zl, xl, c, u
    )
    whole = lax.all_gather(payload, "k")
    piece = jnp.concatenate([whole[:, 96:112], whole[:, 112:128]], 2)
    got = lax.all_to_all(jnp.broadcast_to(piece[None], (8, 8, 16, 512)), "sub", 0, 0, tiled=True)
    core = jnp.concatenate(
        [
            whole[:, 224:240, :BLOCK],
            whole[:, 224:240, BLOCK:],
            whole[:, 240:, :BLOCK],
            whole[:, 240:, BLOCK:],
        ],
        1,
    ).reshape(384, BLOCK)
    columns = whole[:, :224, BLOCK:].reshape(2, 896, BLOCK)
    down, swap = [(0, 1)], [(0, 1), (1, 0)]
    far = lax.ppermute(jnp.concatenate([columns[0], core], 0), "xl", swap)
    one = jnp.where(xl == 0, columns[0], far[:896])
    two = jnp.where(zl == 0, columns[1], lax.ppermute(columns[1], "zl", down))
    cores = jnp.concatenate([core, far[896:]], 0)
    far = lax.ppermute(jnp.concatenate([one, cores], 0), "zl", swap)
    one = jnp.where(zl == 0, one, far[:896])
    two = jnp.where(xl == 0, two, lax.ppermute(two, "xl", down))
    near = jnp.concatenate([one, two, cores, far[896:]], 0)
    other = lax.ppermute(near, "c", swap)
    return upper_levels(info, whole, got, near, other, pivot_entries, pivot_inverse)


def solution(mesh):
    cube = ("k", "zl", "xl", "c")
    split = Mesh(mesh.devices.reshape(8, 2, 2, 2, 8), cube + ("sub",))
    return jax.shard_map(
        local,
        mesh=split,
        in_specs=(P(cube, "sub"), P(), P(), P(), P(), P()),
        out_specs=P(cube, "sub"),
        check_vma=False,
    )
```

```python
import jax
import jax.numpy as jnp
from jax import lax
from jax.experimental import pallas as pl
from jax.experimental.pallas import tpu as pltpu
from jax.sharding import Mesh, PartitionSpec as P

BLOCK = 128
CHUNK = 256
F32 = jnp.float32
BF16 = jnp.bfloat16
CORE_AT = 8 * 224
MAP_START = (3, 3 + 112, 3 + 112 + 120)


def dot(lhs, rhs):
    return jnp.dot(lhs, rhs, preferred_element_type=F32)


def dot_tn(lhs, rhs):
    return lax.dot_general(lhs, rhs, (((0,), (0,)), ((), ())), preferred_element_type=F32)


def panels(first, second, inverse_zero, inverse_one, row_one):
    scaled_zero = dot(inverse_zero, first).astype(BF16)
    coupling = first[:, row_one : row_one + BLOCK]
    col_one = (second.astype(F32) - dot_tn(coupling, scaled_zero)).astype(BF16)
    scaled_one = dot(inverse_one, col_one).astype(BF16)
    columns = jnp.concatenate([first, col_one], 0)
    scaled = jnp.concatenate([scaled_zero, scaled_one], 0)
    return columns, scaled


def upper_kernel(
    info, whole_hbm, got_hbm, near_hbm, other_hbm, pivots, all_inverses, out_hbm,
    z_one, z_two, z_top, y_one, y_two, y_top, t_one, t_two, own_one, own_two, core_one, core_two,
    couplings, top, inverses, whole, got, near, other, out, arrived, left,
):
    p, s, u = info[0], info[1], info[2]
    c = u % 2
    copies = [
        pltpu.make_async_copy(source, target, arrived.at[i])
        for i, (source, target) in enumerate(
            (
                (near_hbm, near),
                (other_hbm, other),
                (whole_hbm, whole),
                (got_hbm, got),
                (all_inverses.at[8:15], inverses),
                (pivots.at[0:7, 0:BLOCK, BLOCK : 2 * BLOCK], couplings),
                (pivots.at[6], top),
            )
        )
    ]
    for copy in copies:
        copy.start()
    for ref in (z_one, y_one, z_two, y_two, z_top, y_top):
        ref[...] = jnp.zeros_like(ref)
    for copy in copies[:3]:
        copy.wait()
    z_refs = (None, z_one, z_two, z_top)
    y_refs = (None, y_one, y_two, y_top)
    t_refs = (None, t_one, t_two)
    own_refs = (None, own_one, own_two)
    core_refs = (None, core_one, core_two)

    def entry(level, front, child, index):
        count = (8 << level) - 2
        return info[MAP_START[level - 1] + (front * 2 + child) * count + index]

    def find(level, front, child, wanted):
        group = 4 << level
        low = lax.rem(p, group)
        first = entry(level, front, child, jnp.maximum(low - 2, 0))
        second = entry(level, front, child, low + group - 2)
        spot = jnp.where(second == wanted, low + group, -1)
        return jnp.where((low >= 2) & (first == wanted), low, spot)

    slots = {(3, 0): [p, p + 64]}
    for level in (3, 2, 1):
        for front in range(16 >> level):
            slots[level - 1, front] = [
                find(level, front // 2, front % 2, spot) for spot in slots[level, front // 2]
            ]

    def leaf_slots(front, wide):
        parts = []
        for spot in slots[0, front]:
            part = jnp.where(spot >= 8, wide[:, BLOCK:], wide[:, :BLOCK])
            parts.append(jnp.where(spot >= 0, part, jnp.zeros_like(part)))
        return jnp.concatenate(parts, 1)

    def stacked(front, lanes):
        return jnp.concatenate([got[sub, front, :, lanes] for sub in range(8)], 0)

    def leaf_own(front, q):
        return leaf_slots(front, stacked(front, slice(256 * q, 256 * q + 256)))

    def share(other_u, front, part):
        apart = u ^ other_u
        start = CORE_AT + apart // 2 * 384 + front * 48 + part * 16
        at = pl.ds(pl.multiple_of(start, 16), 16)
        return jnp.where(apart % 2 == 0, near[at, :], other[at, :])

    def leaf_core(front):
        blocks = [
            jnp.concatenate([share(member, front, part) for member in range(8)], 0)
            for part in range(3)
        ]
        turned = blocks[1].astype(F32).T.astype(BF16)
        return jnp.concatenate(blocks[:2], 1), jnp.concatenate([turned, blocks[2]], 1)

    for level in (1, 2, 3):
        z_ref, y_ref = z_refs[level], y_refs[level]
        group = 4 << level
        width = 256 << level
        wanted = 4 if level < 3 else 2
        panels_t = []
        for front in range(8 >> level):
            kids = (2 * front, 2 * front + 1)
            goal = (0, 1, 2 * group, 2 * group + 1)
            mask = [
                [entry(level, front, child, group - 2 + q % 2) == goal[q] for q in range(4)]
                for child in range(2)
            ]

            def masked(child, q, value):
                return jnp.where(mask[child][q], value, jnp.zeros_like(value))

            for child, kid in enumerate(kids):
                def put(block, dest, panel, row):
                    spread = [
                        masked(child, q, panel[:, (q % 2) * BLOCK : (q % 2 + 1) * BLOCK])
                        for q in range(wanted)
                    ]
                    spread = jnp.concatenate(spread, 1)
                    at = pl.ds(pl.multiple_of(dest * 16, 16), 16)
                    if child == 1:
                        spread = spread + z_ref[front, at, :]
                        row = row + y_ref[front, at, :]
                    z_ref[front, at, :] = spread
                    y_ref[front, at, :] = row

                if level == 1:
                    for block in range(2, 16):
                        at = slice(16 * (block - 2), 16 * (block - 1))
                        start = kid * 224 + 16 * (block - 2)
                        one, two = near[start : start + 16, :], other[start : start + 16, :]
                        panel = jnp.concatenate(
                            [jnp.where(c == 0, one, two), jnp.where(c == 0, two, one)], 1
                        )
                        row = leaf_slots(kid, whole[kid, at, :])
                        put(block, entry(level, front, child, block - 2), panel, row)
                else:
                    def step(block, carry):
                        at = pl.ds(pl.multiple_of(block * 16, 16), 16)
                        put(
                            block,
                            entry(level, front, child, block - 2),
                            t_refs[level - 1][kid, at, :],
                            y_refs[level - 1][kid, at, :],
                        )
                        return carry

                    lax.fori_loop(2, 2 * group, step, 0, unroll=6)

            if level == 3:
                for half in range(2):
                    at = pl.ds(pl.multiple_of(half * BLOCK + 16 * s, 16), 16)
                    strip = top[at, :]
                    z_ref[0, 16 * half : 16 * half + 16, :] += strip
                    strip = jnp.where(p == 0, strip[:, :BLOCK], strip[:, BLOCK:])
                    strip = jnp.where(p < 2, strip, jnp.zeros_like(strip))
                    y_ref[0, 16 * half : 16 * half + 16, :BLOCK] += strip

            core_rows = (2, 3, 1) if level < 3 else (1,)
            if level == 1 and front == 0:
                for copy in copies[3:]:
                    copy.wait()
            if level == 1:
                kid_own = [[leaf_own(kid, q) for q in range(2)] for kid in kids]
                kid_core = [leaf_core(kid) for kid in kids]
            zt = []
            for q in range(wanted):
                parts = []
                own = jnp.zeros((BLOCK, 256), F32)
                for child, kid in enumerate(kids):
                    if level == 1:
                        value = kid_own[child][q % 2]
                    else:
                        value = own_refs[level - 1][kid, (q % 2) * BLOCK : (q % 2 + 1) * BLOCK, :]
                    own = own + masked(child, q, value.astype(F32))
                if level == 3:
                    strip = top[q * BLOCK : (q + 1) * BLOCK, :].astype(F32)
                    strip = jnp.where(p == 0, strip[:, :BLOCK], strip[:, BLOCK:])
                    strip = jnp.where(p < 2, strip, jnp.zeros_like(strip))
                    own = own + jnp.concatenate([strip, jnp.zeros_like(strip)], 1)
                parts.append(own)
                for r in core_rows:
                    value = jnp.zeros((BLOCK, BLOCK), F32)
                    for child, kid in enumerate(kids):
                        if level == 1:
                            part = kid_core[child][q % 2]
                        else:
                            part = core_refs[level - 1][kid, (q % 2) * BLOCK : (q % 2 + 1) * BLOCK, :]
                        part = part[:, (r % 2) * BLOCK : (r % 2 + 1) * BLOCK].astype(F32)
                        value = value + masked(child, q, masked(child, r, part))
                    if q == 0 and r == 1:
                        value = value + couplings[8 - (16 >> level) + front].astype(F32)
                    parts.append(value)
                zt.append(jnp.concatenate(parts, 1).astype(BF16))
            panels_t.append(zt)

        fronts = range(8 >> level)
        pieces = [(front, start) for front in fronts for start in range(0, width, CHUNK)]
        live = panels_t[0][0].shape[1] - BLOCK
        inverse = [
            [inverses[8 - (16 >> level) + front, q] for q in range(2)] for front in fronts
        ]

        def rows_of(ref, front, start, q):
            return ref[front, pl.ds(start, CHUNK), q * BLOCK : (q + 1) * BLOCK]

        scaled_zero_t = [dot(inverse[f][0], panels_t[f][0]).astype(BF16) for f in fronts]
        scaled_zero = [dot(rows_of(z_ref, f, at, 0), inverse[f][0]).astype(BF16) for f, at in pieces]
        second_t, second = [], []
        for f in fronts:
            coupling = panels_t[f][0][:, live:]
            value = panels_t[f][1].astype(F32) - dot_tn(coupling, scaled_zero_t[f])
            second_t.append(value.astype(BF16))
        for i, (f, at) in enumerate(pieces):
            coupling = panels_t[f][0][:, live:]
            value = rows_of(z_ref, f, at, 1).astype(F32) - dot(scaled_zero[i], coupling)
            second.append(value.astype(BF16))
        scaled_one_t = [dot(inverse[f][1], second_t[f]).astype(BF16) for f in fronts]
        if level < 3:
            scaled_one = [dot(second[i], inverse[f][1]).astype(BF16) for i, (f, _) in enumerate(pieces)]
            core_cols = [
                jnp.concatenate([panels_t[f][0][:, 256:512], second_t[f][:, 256:512]], 0)
                for f in fronts
            ]
            for f in fronts:
                later = jnp.concatenate([panels_t[f][2], panels_t[f][3]], 0)[:, :512].astype(F32)
                scaled = jnp.concatenate([scaled_zero_t[f][:, :512], scaled_one_t[f][:, :512]], 0)
                later = (later - dot_tn(core_cols[f], scaled)).astype(BF16)
                own_refs[level][f] = later[:, :256]
                core_refs[level][f] = later[:, 256:]
        for i, (f, at) in enumerate(pieces):
            own_scaled = jnp.concatenate([scaled_zero_t[f][:, :256], scaled_one_t[f][:, :256]], 0)
            columns = jnp.concatenate([rows_of(z_ref, f, at, 0), second[i]], 1)
            row = y_ref[f, pl.ds(at, CHUNK), :].astype(F32) - dot(columns, own_scaled)
            if level == 3:
                out[i] = row.T.astype(BF16)
                copy = pltpu.make_async_copy(
                    out.at[i], out_hbm.at[:, pl.ds(at, CHUNK)], left.at[i]
                )
                copy.start()
                copies.append(copy)
                continue
            y_ref[f, pl.ds(at, CHUNK), :] = row.astype(BF16)
            rest = z_ref[f, pl.ds(at, CHUNK), 2 * BLOCK :].astype(F32)
            rest = rest - dot(jnp.concatenate([scaled_zero[i], scaled_one[i]], 1), core_cols[f])
            t_refs[level][f, pl.ds(at, CHUNK), :] = rest.astype(BF16)
    for copy in copies[7:]:
        copy.wait()


def upper_levels(info, whole, got, near, other, pivots, inverses):
    anywhere = pl.BlockSpec(memory_space=pltpu.HBM)
    return pl.pallas_call(
        upper_kernel,
        out_shape=jax.ShapeDtypeStruct((256, 2048), BF16),
        in_specs=[pl.BlockSpec(memory_space=pltpu.SMEM)] + [pl.BlockSpec(memory_space=pl.ANY)] * 4 + [anywhere] * 2,
        out_specs=anywhere,
        scratch_shapes=[
            pltpu.VMEM(shape, BF16)
            for shape in (
                (4, 512, 512), (2, 1024, 512), (1, 2048, 256),
                (4, 512, 256), (2, 1024, 256), (1, 2048, 256),
                (4, 512, 256), (2, 1024, 256),
                (4, 256, 256), (2, 256, 256), (4, 256, 256), (2, 256, 256),
                (7, BLOCK, BLOCK), (256, 256), (7, 2, BLOCK, BLOCK),
                whole.shape, got.shape, near.shape, other.shape, (8, 256, CHUNK),
            )
        ]
        + [pltpu.SemaphoreType.DMA((7,)), pltpu.SemaphoreType.DMA((8,))],
        compiler_params=pltpu.CompilerParams(vmem_limit_bytes=62 * 2**20),
        name="upper_levels",
    )(info, whole, got, near, other, pivots, inverses)


def leaf_stage(leaf, inverses, zl, xl, c, u):
    tile = leaf
    spread = jnp.where(xl == 0, tile, lax.ppermute(tile, "xl", [(0, 1)]))
    spread = jnp.where(zl == 0, spread, lax.ppermute(spread, "zl", [(0, 1)]))
    other = lax.ppermute(spread, "c", [(0, 1), (1, 0)])
    even = jnp.where(c == 0, spread, other)
    odd = jnp.where(c == 0, other, spread)
    piece = jnp.concatenate(
        [
            tile[:, :32],
            odd[:BLOCK, :32],
            even[BLOCK:, :32],
            odd[BLOCK:, :32],
            even[BLOCK:, 128:160],
            odd[BLOCK:, 128:160],
        ],
        0,
    ).T
    got = lax.all_to_all(jnp.broadcast_to(piece[None], (8,) + piece.shape), "sub", 0, 0, tiled=True)
    got = got.reshape(8, 2, 16, 896).transpose(1, 0, 2, 3).reshape(2, BLOCK, 896)
    first = jnp.concatenate([even[:BLOCK], got[0, :, :640]], 1)
    second = jnp.concatenate([odd[:BLOCK], got[1, :, :640]], 1)
    columns, scaled = panels(first, second, inverses[0], inverses[1], 512)
    core = got[:, :, 640:].reshape(256, 256).astype(F32)
    core = core - dot_tn(columns[:, 640:], scaled[:, 640:])
    core = core.astype(BF16)
    upper = lax.dynamic_slice_in_dim(core[:BLOCK], 16 * u, 16, 0)
    lower = lax.dynamic_slice_in_dim(core[BLOCK:, BLOCK:], 16 * u, 16, 0)
    tile = tile.T.astype(F32) - dot_tn(columns[:, :256], scaled[:, 256:512])
    return jnp.concatenate(
        [tile[32:].astype(BF16), upper, jnp.concatenate([lower[:8], lower[8:]], 1)], 0
    )


def local(leaf_fronts, pivot_entries, pivot_inverse, block_map_one, block_map_two, block_map_top):
    k, zl, xl, c = (lax.axis_index(name) for name in ("k", "zl", "xl", "c"))
    s = lax.axis_index("sub")
    u = zl * 4 + xl * 2 + c
    maps = (block_map_one, block_map_two, block_map_top)
    info = jnp.concatenate(
        [jnp.stack([k * 8 + u, s, u]).astype(jnp.int32)] + [table.reshape(-1) for table in maps]
    )
    payload = leaf_stage(
        leaf_fronts, lax.dynamic_index_in_dim(pivot_inverse, k, 0, keepdims=False), zl, xl, c, u
    )
    whole = lax.all_gather(payload, "k")
    piece = jnp.concatenate([whole[:, 96:112], whole[:, 112:128]], 2)
    got = lax.all_to_all(jnp.broadcast_to(piece[None], (8, 8, 16, 512)), "sub", 0, 0, tiled=True)
    core = jnp.concatenate(
        [
            whole[:, 224:240, :BLOCK],
            whole[:, 224:240, BLOCK:],
            whole[:, 240:, :BLOCK],
            whole[:, 240:, BLOCK:],
        ],
        1,
    ).reshape(384, BLOCK)
    columns = whole[:, :224, BLOCK:].reshape(2, 896, BLOCK)
    down, swap = [(0, 1)], [(0, 1), (1, 0)]
    far = lax.ppermute(jnp.concatenate([columns[0], core], 0), "xl", swap)
    one = jnp.where(xl == 0, columns[0], far[:896])
    two = jnp.where(zl == 0, columns[1], lax.ppermute(columns[1], "zl", down))
    cores = jnp.concatenate([core, far[896:]], 0)
    far = lax.ppermute(jnp.concatenate([one, cores], 0), "zl", swap)
    one = jnp.where(zl == 0, one, far[:896])
    two = jnp.where(xl == 0, two, lax.ppermute(two, "xl", down))
    near = jnp.concatenate([one, two, cores, far[896:]], 0)
    other = lax.ppermute(near, "c", swap)
    return upper_levels(info, whole, got, near, other, pivot_entries, pivot_inverse)


def solution(mesh):
    cube = ("k", "zl", "xl", "c")
    split = Mesh(mesh.devices.reshape(8, 2, 2, 2, 8), cube + ("sub",))
    return jax.shard_map(
        local,
        mesh=split,
        in_specs=(P(cube, "sub"), P(), P(), P(), P(), P()),
        out_specs=P(cube, "sub"),
        check_vma=False,
    )
```

```python
import jax
import jax.numpy as jnp
from jax import lax
from jax.experimental import pallas as pl
from jax.experimental.pallas import tpu as pltpu
from jax.sharding import Mesh, PartitionSpec as P

BLOCK = 128
CHUNK = 256
F32 = jnp.float32
BF16 = jnp.bfloat16
CORE_AT = 8 * 224
SPLIT = 6 * 224
MAP_START = (3, 3 + 112, 3 + 112 + 120)


def dot(lhs, rhs):
    return jnp.dot(lhs, rhs, preferred_element_type=F32)


def dot_tn(lhs, rhs):
    return lax.dot_general(lhs, rhs, (((0,), (0,)), ((), ())), preferred_element_type=F32)


def panels(first, second, inverse_zero, inverse_one, row_one):
    scaled_zero = dot(inverse_zero, first).astype(BF16)
    coupling = first[:, row_one : row_one + BLOCK]
    col_one = (second.astype(F32) - dot_tn(coupling, scaled_zero)).astype(BF16)
    scaled_one = dot(inverse_one, col_one).astype(BF16)
    columns = jnp.concatenate([first, col_one], 0)
    scaled = jnp.concatenate([scaled_zero, scaled_one], 0)
    return columns, scaled


def upper_kernel(
    info, whole_hbm, got_hbm, near_hbm, other_hbm, pivots, all_inverses, out_hbm,
    z_one, z_two, z_top, y_one, y_two, y_top, t_one, t_two, own_one, own_two, core_one, core_two,
    couplings, top, inverses, whole, got, near, other, out, arrived, left,
):
    p, s, u = info[0], info[1], info[2]
    c = u % 2
    copies = [
        pltpu.make_async_copy(source, target, arrived.at[i])
        for i, (source, target) in enumerate(
            (
                (near_hbm, near),
                (other_hbm, other),
                (whole_hbm, whole),
                (got_hbm, got),
                (all_inverses.at[8:15], inverses),
                (pivots.at[0:7, 0:BLOCK, BLOCK : 2 * BLOCK], couplings),
                (pivots.at[6], top),
            )
        )
    ]
    for copy in copies:
        copy.start()
    for ref in (z_one, y_one, z_two, y_two, z_top, y_top):
        ref[...] = jnp.zeros_like(ref)
    for copy in copies[:3]:
        copy.wait()
    z_refs = (None, z_one, z_two, z_top)
    y_refs = (None, y_one, y_two, y_top)
    t_refs = (None, t_one, t_two)
    own_refs = (None, own_one, own_two)
    core_refs = (None, core_one, core_two)

    def entry(level, front, child, index):
        count = (8 << level) - 2
        return info[MAP_START[level - 1] + (front * 2 + child) * count + index]

    def find(level, front, child, wanted):
        group = 4 << level
        low = lax.rem(p, group)
        first = entry(level, front, child, jnp.maximum(low - 2, 0))
        second = entry(level, front, child, low + group - 2)
        spot = jnp.where(second == wanted, low + group, -1)
        return jnp.where((low >= 2) & (first == wanted), low, spot)

    slots = {(3, 0): [p, p + 64]}
    for level in (3, 2, 1):
        for front in range(16 >> level):
            slots[level - 1, front] = [
                find(level, front // 2, front % 2, spot) for spot in slots[level, front // 2]
            ]

    def leaf_slots(front, wide):
        parts = []
        for spot in slots[0, front]:
            part = jnp.where(spot >= 8, wide[:, BLOCK:], wide[:, :BLOCK])
            parts.append(jnp.where(spot >= 0, part, jnp.zeros_like(part)))
        return jnp.concatenate(parts, 1)

    def stacked(front, lanes):
        return jnp.concatenate([got[sub, front, :, lanes] for sub in range(8)], 0)

    def leaf_own(front, q):
        return leaf_slots(front, stacked(front, slice(256 * q, 256 * q + 256)))

    def share(other_u, front, part):
        apart = u ^ other_u
        start = CORE_AT + apart // 2 * 384 + front * 48 + part * 16
        at = pl.ds(pl.multiple_of(start, 16), 16)
        return jnp.where(apart % 2 == 0, near[at, :], other[at, :])

    def leaf_core(front):
        blocks = [
            jnp.concatenate([share(member, front, part) for member in range(8)], 0)
            for part in range(3)
        ]
        turned = blocks[1].astype(F32).T.astype(BF16)
        return jnp.concatenate(blocks[:2], 1), jnp.concatenate([turned, blocks[2]], 1)

    for level in (1, 2, 3):
        z_ref, y_ref = z_refs[level], y_refs[level]
        group = 4 << level
        width = 256 << level
        wanted = 4 if level < 3 else 2
        panels_t = []
        for front in range(8 >> level):
            kids = (2 * front, 2 * front + 1)
            goal = (0, 1, 2 * group, 2 * group + 1)
            mask = [
                [entry(level, front, child, group - 2 + q % 2) == goal[q] for q in range(4)]
                for child in range(2)
            ]

            def masked(child, q, value):
                return jnp.where(mask[child][q], value, jnp.zeros_like(value))

            for child, kid in enumerate(kids):
                def put(block, dest, panel, row):
                    spread = [
                        masked(child, q, panel[:, (q % 2) * BLOCK : (q % 2 + 1) * BLOCK])
                        for q in range(wanted)
                    ]
                    spread = jnp.concatenate(spread, 1)
                    at = pl.ds(pl.multiple_of(dest * 16, 16), 16)
                    if child == 1:
                        spread = spread + z_ref[front, at, :]
                        row = row + y_ref[front, at, :]
                    z_ref[front, at, :] = spread
                    y_ref[front, at, :] = row

                if level == 1:
                    for block in range(2, 16):
                        at = slice(16 * (block - 2), 16 * (block - 1))
                        start = kid * 224 + 16 * (block - 2)
                        one, two = near[start : start + 16, :], other[start : start + 16, :]
                        panel = jnp.concatenate(
                            [jnp.where(c == 0, one, two), jnp.where(c == 0, two, one)], 1
                        )
                        row = leaf_slots(kid, whole[kid, at, :])
                        put(block, entry(level, front, child, block - 2), panel, row)
                else:
                    def step(block, carry):
                        at = pl.ds(pl.multiple_of(block * 16, 16), 16)
                        put(
                            block,
                            entry(level, front, child, block - 2),
                            t_refs[level - 1][kid, at, :],
                            y_refs[level - 1][kid, at, :],
                        )
                        return carry

                    lax.fori_loop(2, 2 * group, step, 0, unroll=6)

            if level == 3:
                for half in range(2):
                    at = pl.ds(pl.multiple_of(half * BLOCK + 16 * s, 16), 16)
                    strip = top[at, :]
                    z_ref[0, 16 * half : 16 * half + 16, :] += strip
                    strip = jnp.where(p == 0, strip[:, :BLOCK], strip[:, BLOCK:])
                    strip = jnp.where(p < 2, strip, jnp.zeros_like(strip))
                    y_ref[0, 16 * half : 16 * half + 16, :BLOCK] += strip

            core_rows = (2, 3, 1) if level < 3 else (1,)
            if level == 1 and front == 0:
                for copy in copies[3:]:
                    copy.wait()
            if level == 1:
                kid_own = [[leaf_own(kid, q) for q in range(2)] for kid in kids]
                kid_core = [leaf_core(kid) for kid in kids]
            zt = []
            for q in range(wanted):
                parts = []
                own = jnp.zeros((BLOCK, 256), F32)
                for child, kid in enumerate(kids):
                    if level == 1:
                        value = kid_own[child][q % 2]
                    else:
                        value = own_refs[level - 1][kid, (q % 2) * BLOCK : (q % 2 + 1) * BLOCK, :]
                    own = own + masked(child, q, value.astype(F32))
                if level == 3:
                    strip = top[q * BLOCK : (q + 1) * BLOCK, :].astype(F32)
                    strip = jnp.where(p == 0, strip[:, :BLOCK], strip[:, BLOCK:])
                    strip = jnp.where(p < 2, strip, jnp.zeros_like(strip))
                    own = own + jnp.concatenate([strip, jnp.zeros_like(strip)], 1)
                parts.append(own)
                for r in core_rows:
                    value = jnp.zeros((BLOCK, BLOCK), F32)
                    for child, kid in enumerate(kids):
                        if level == 1:
                            part = kid_core[child][q % 2]
                        else:
                            part = core_refs[level - 1][kid, (q % 2) * BLOCK : (q % 2 + 1) * BLOCK, :]
                        part = part[:, (r % 2) * BLOCK : (r % 2 + 1) * BLOCK].astype(F32)
                        value = value + masked(child, q, masked(child, r, part))
                    if q == 0 and r == 1:
                        value = value + couplings[8 - (16 >> level) + front].astype(F32)
                    parts.append(value)
                zt.append(jnp.concatenate(parts, 1).astype(BF16))
            panels_t.append(zt)

        fronts = range(8 >> level)
        pieces = [(front, start) for front in fronts for start in range(0, width, CHUNK)]
        live = panels_t[0][0].shape[1] - BLOCK
        inverse = [
            [inverses[8 - (16 >> level) + front, q] for q in range(2)] for front in fronts
        ]

        def rows_of(ref, front, start, q):
            return ref[front, pl.ds(start, CHUNK), q * BLOCK : (q + 1) * BLOCK]

        scaled_zero_t = [dot(inverse[f][0], panels_t[f][0]).astype(BF16) for f in fronts]
        scaled_zero = [dot(rows_of(z_ref, f, at, 0), inverse[f][0]).astype(BF16) for f, at in pieces]
        second_t, second = [], []
        for f in fronts:
            coupling = panels_t[f][0][:, live:]
            value = panels_t[f][1].astype(F32) - dot_tn(coupling, scaled_zero_t[f])
            second_t.append(value.astype(BF16))
        for i, (f, at) in enumerate(pieces):
            coupling = panels_t[f][0][:, live:]
            value = rows_of(z_ref, f, at, 1).astype(F32) - dot(scaled_zero[i], coupling)
            second.append(value.astype(BF16))
        scaled_one_t = [dot(inverse[f][1], second_t[f]).astype(BF16) for f in fronts]
        if level < 3:
            scaled_one = [dot(second[i], inverse[f][1]).astype(BF16) for i, (f, _) in enumerate(pieces)]
            core_cols = [
                jnp.concatenate([panels_t[f][0][:, 256:512], second_t[f][:, 256:512]], 0)
                for f in fronts
            ]
            for f in fronts:
                later = jnp.concatenate([panels_t[f][2], panels_t[f][3]], 0)[:, :512].astype(F32)
                scaled = jnp.concatenate([scaled_zero_t[f][:, :512], scaled_one_t[f][:, :512]], 0)
                later = (later - dot_tn(core_cols[f], scaled)).astype(BF16)
                own_refs[level][f] = later[:, :256]
                core_refs[level][f] = later[:, 256:]
        for i, (f, at) in enumerate(pieces):
            own_scaled = jnp.concatenate([scaled_zero_t[f][:, :256], scaled_one_t[f][:, :256]], 0)
            columns = jnp.concatenate([rows_of(z_ref, f, at, 0), second[i]], 1)
            row = y_ref[f, pl.ds(at, CHUNK), :].astype(F32) - dot(columns, own_scaled)
            if level == 3:
                out[i] = row.T.astype(BF16)
                copy = pltpu.make_async_copy(
                    out.at[i], out_hbm.at[:, pl.ds(at, CHUNK)], left.at[i]
                )
                copy.start()
                copies.append(copy)
                continue
            y_ref[f, pl.ds(at, CHUNK), :] = row.astype(BF16)
            rest = z_ref[f, pl.ds(at, CHUNK), 2 * BLOCK :].astype(F32)
            rest = rest - dot(jnp.concatenate([scaled_zero[i], scaled_one[i]], 1), core_cols[f])
            t_refs[level][f, pl.ds(at, CHUNK), :] = rest.astype(BF16)
    for copy in copies[7:]:
        copy.wait()


def upper_levels(info, whole, got, near, other, pivots, inverses):
    anywhere = pl.BlockSpec(memory_space=pltpu.HBM)
    return pl.pallas_call(
        upper_kernel,
        out_shape=jax.ShapeDtypeStruct((256, 2048), BF16),
        in_specs=[pl.BlockSpec(memory_space=pltpu.SMEM)] + [pl.BlockSpec(memory_space=pl.ANY)] * 4 + [anywhere] * 2,
        out_specs=anywhere,
        scratch_shapes=[
            pltpu.VMEM(shape, BF16)
            for shape in (
                (4, 512, 512), (2, 1024, 512), (1, 2048, 256),
                (4, 512, 256), (2, 1024, 256), (1, 2048, 256),
                (4, 512, 256), (2, 1024, 256),
                (4, 256, 256), (2, 256, 256), (4, 256, 256), (2, 256, 256),
                (7, BLOCK, BLOCK), (256, 256), (7, 2, BLOCK, BLOCK),
                whole.shape, got.shape, near.shape, other.shape, (8, 256, CHUNK),
            )
        ]
        + [pltpu.SemaphoreType.DMA((7,)), pltpu.SemaphoreType.DMA((8,))],
        compiler_params=pltpu.CompilerParams(vmem_limit_bytes=62 * 2**20),
        name="upper_levels",
    )(info, whole, got, near, other, pivots, inverses)


def leaf_stage(leaf, inverses, zl, xl, c, u):
    tile = leaf
    spread = jnp.where(xl == 0, tile, lax.ppermute(tile, "xl", [(0, 1)]))
    spread = jnp.where(zl == 0, spread, lax.ppermute(spread, "zl", [(0, 1)]))
    other = lax.ppermute(spread, "c", [(0, 1), (1, 0)])
    even = jnp.where(c == 0, spread, other)
    odd = jnp.where(c == 0, other, spread)
    piece = jnp.concatenate(
        [
            tile[:, :32],
            odd[:BLOCK, :32],
            even[BLOCK:, :32],
            odd[BLOCK:, :32],
            even[BLOCK:, 128:160],
            odd[BLOCK:, 128:160],
        ],
        0,
    ).T
    got = lax.all_to_all(jnp.broadcast_to(piece[None], (8,) + piece.shape), "sub", 0, 0, tiled=True)
    got = got.reshape(8, 2, 16, 896).transpose(1, 0, 2, 3).reshape(2, BLOCK, 896)
    first = jnp.concatenate([even[:BLOCK], got[0, :, :640]], 1)
    second = jnp.concatenate([odd[:BLOCK], got[1, :, :640]], 1)
    columns, scaled = panels(first, second, inverses[0], inverses[1], 512)
    core = got[:, :, 640:].reshape(256, 256).astype(F32)
    core = core - dot_tn(columns[:, 640:], scaled[:, 640:])
    core = core.astype(BF16)
    upper = lax.dynamic_slice_in_dim(core[:BLOCK], 16 * u, 16, 0)
    lower = lax.dynamic_slice_in_dim(core[BLOCK:, BLOCK:], 16 * u, 16, 0)
    tile = tile.T.astype(F32) - dot_tn(columns[:, :256], scaled[:, 256:512])
    return jnp.concatenate(
        [tile[32:].astype(BF16), upper, jnp.concatenate([lower[:8], lower[8:]], 1)], 0
    )


def local(leaf_fronts, pivot_entries, pivot_inverse, block_map_one, block_map_two, block_map_top):
    k, zl, xl, c = (lax.axis_index(name) for name in ("k", "zl", "xl", "c"))
    s = lax.axis_index("sub")
    u = zl * 4 + xl * 2 + c
    maps = (block_map_one, block_map_two, block_map_top)
    info = jnp.concatenate(
        [jnp.stack([k * 8 + u, s, u]).astype(jnp.int32)] + [table.reshape(-1) for table in maps]
    )
    payload = leaf_stage(
        leaf_fronts, lax.dynamic_index_in_dim(pivot_inverse, k, 0, keepdims=False), zl, xl, c, u
    )
    whole = lax.all_gather(payload, "k")
    piece = jnp.concatenate([whole[:, 96:112], whole[:, 112:128]], 2)
    got = lax.all_to_all(jnp.broadcast_to(piece[None], (8, 8, 16, 512)), "sub", 0, 0, tiled=True)
    core = jnp.concatenate(
        [
            whole[:, 224:240, :BLOCK],
            whole[:, 224:240, BLOCK:],
            whole[:, 240:, :BLOCK],
            whole[:, 240:, BLOCK:],
        ],
        1,
    ).reshape(384, BLOCK)
    columns = whole[:, :224, BLOCK:].reshape(CORE_AT, BLOCK)
    first, second = columns[:SPLIT], columns[SPLIT:]
    down, swap = [(0, 1)], [(0, 1), (1, 0)]
    far = lax.ppermute(jnp.concatenate([first, core], 0), "xl", swap)
    one = jnp.where(xl == 0, first, far[:SPLIT])
    two = jnp.where(zl == 0, second, lax.ppermute(second, "zl", down))
    cores = jnp.concatenate([core, far[SPLIT:]], 0)
    far = lax.ppermute(jnp.concatenate([one, cores], 0), "zl", swap)
    one = jnp.where(zl == 0, one, far[:SPLIT])
    two = jnp.where(xl == 0, two, lax.ppermute(two, "xl", down))
    near = jnp.concatenate([one, two, cores, far[SPLIT:]], 0)
    other = lax.ppermute(near, "c", swap)
    return upper_levels(info, whole, got, near, other, pivot_entries, pivot_inverse)


def solution(mesh):
    cube = ("k", "zl", "xl", "c")
    split = Mesh(mesh.devices.reshape(8, 2, 2, 2, 8), cube + ("sub",))
    return jax.shard_map(
        local,
        mesh=split,
        in_specs=(P(cube, "sub"), P(), P(), P(), P(), P()),
        out_specs=P(cube, "sub"),
        check_vma=False,
    )
```

```python
import jax
import jax.numpy as jnp
from jax import lax
from jax.experimental import pallas as pl
from jax.experimental.pallas import tpu as pltpu
from jax.sharding import Mesh, PartitionSpec as P

BLOCK = 128
CHUNK = 256
F32 = jnp.float32
BF16 = jnp.bfloat16
CORE_AT = 8 * 224
SPLIT = 7 * 224
MAP_START = (3, 3 + 112, 3 + 112 + 120)


def dot(lhs, rhs):
    return jnp.dot(lhs, rhs, preferred_element_type=F32)


def dot_tn(lhs, rhs):
    return lax.dot_general(lhs, rhs, (((0,), (0,)), ((), ())), preferred_element_type=F32)


def panels(first, second, inverse_zero, inverse_one, row_one):
    scaled_zero = dot(inverse_zero, first).astype(BF16)
    coupling = first[:, row_one : row_one + BLOCK]
    col_one = (second.astype(F32) - dot_tn(coupling, scaled_zero)).astype(BF16)
    scaled_one = dot(inverse_one, col_one).astype(BF16)
    columns = jnp.concatenate([first, col_one], 0)
    scaled = jnp.concatenate([scaled_zero, scaled_one], 0)
    return columns, scaled


def upper_kernel(
    info, whole_hbm, got_hbm, near_hbm, other_hbm, pivots, all_inverses, out_hbm,
    z_one, z_two, z_top, y_one, y_two, y_top, t_one, t_two, own_one, own_two, core_one, core_two,
    couplings, top, inverses, whole, got, near, other, out, arrived, left,
):
    p, s, u = info[0], info[1], info[2]
    c = u % 2
    copies = [
        pltpu.make_async_copy(source, target, arrived.at[i])
        for i, (source, target) in enumerate(
            (
                (near_hbm, near),
                (other_hbm, other),
                (whole_hbm, whole),
                (got_hbm, got),
                (all_inverses.at[8:15], inverses),
                (pivots.at[0:7, 0:BLOCK, BLOCK : 2 * BLOCK], couplings),
                (pivots.at[6], top),
            )
        )
    ]
    for copy in copies:
        copy.start()
    for ref in (z_one, y_one, z_two, y_two, z_top, y_top):
        ref[...] = jnp.zeros_like(ref)
    for copy in copies[:3]:
        copy.wait()
    z_refs = (None, z_one, z_two, z_top)
    y_refs = (None, y_one, y_two, y_top)
    t_refs = (None, t_one, t_two)
    own_refs = (None, own_one, own_two)
    core_refs = (None, core_one, core_two)

    def entry(level, front, child, index):
        count = (8 << level) - 2
        return info[MAP_START[level - 1] + (front * 2 + child) * count + index]

    def find(level, front, child, wanted):
        group = 4 << level
        low = lax.rem(p, group)
        first = entry(level, front, child, jnp.maximum(low - 2, 0))
        second = entry(level, front, child, low + group - 2)
        spot = jnp.where(second == wanted, low + group, -1)
        return jnp.where((low >= 2) & (first == wanted), low, spot)

    slots = {(3, 0): [p, p + 64]}
    for level in (3, 2, 1):
        for front in range(16 >> level):
            slots[level - 1, front] = [
                find(level, front // 2, front % 2, spot) for spot in slots[level, front // 2]
            ]

    def leaf_slots(front, wide):
        parts = []
        for spot in slots[0, front]:
            part = jnp.where(spot >= 8, wide[:, BLOCK:], wide[:, :BLOCK])
            parts.append(jnp.where(spot >= 0, part, jnp.zeros_like(part)))
        return jnp.concatenate(parts, 1)

    def stacked(front, lanes):
        return jnp.concatenate([got[sub, front, :, lanes] for sub in range(8)], 0)

    def leaf_own(front, q):
        return leaf_slots(front, stacked(front, slice(256 * q, 256 * q + 256)))

    def share(other_u, front, part):
        apart = u ^ other_u
        start = CORE_AT + apart // 2 * 384 + front * 48 + part * 16
        at = pl.ds(pl.multiple_of(start, 16), 16)
        return jnp.where(apart % 2 == 0, near[at, :], other[at, :])

    def leaf_core(front):
        blocks = [
            jnp.concatenate([share(member, front, part) for member in range(8)], 0)
            for part in range(3)
        ]
        turned = blocks[1].astype(F32).T.astype(BF16)
        return jnp.concatenate(blocks[:2], 1), jnp.concatenate([turned, blocks[2]], 1)

    for level in (1, 2, 3):
        z_ref, y_ref = z_refs[level], y_refs[level]
        group = 4 << level
        width = 256 << level
        wanted = 4 if level < 3 else 2
        panels_t = []
        for front in range(8 >> level):
            kids = (2 * front, 2 * front + 1)
            goal = (0, 1, 2 * group, 2 * group + 1)
            mask = [
                [entry(level, front, child, group - 2 + q % 2) == goal[q] for q in range(4)]
                for child in range(2)
            ]

            def masked(child, q, value):
                return jnp.where(mask[child][q], value, jnp.zeros_like(value))

            for child, kid in enumerate(kids):
                def put(block, dest, panel, row):
                    spread = [
                        masked(child, q, panel[:, (q % 2) * BLOCK : (q % 2 + 1) * BLOCK])
                        for q in range(wanted)
                    ]
                    spread = jnp.concatenate(spread, 1)
                    at = pl.ds(pl.multiple_of(dest * 16, 16), 16)
                    if child == 1:
                        spread = spread + z_ref[front, at, :]
                        row = row + y_ref[front, at, :]
                    z_ref[front, at, :] = spread
                    y_ref[front, at, :] = row

                if level == 1:
                    for block in range(2, 16):
                        at = slice(16 * (block - 2), 16 * (block - 1))
                        start = kid * 224 + 16 * (block - 2)
                        one, two = near[start : start + 16, :], other[start : start + 16, :]
                        panel = jnp.concatenate(
                            [jnp.where(c == 0, one, two), jnp.where(c == 0, two, one)], 1
                        )
                        row = leaf_slots(kid, whole[kid, at, :])
                        put(block, entry(level, front, child, block - 2), panel, row)
                else:
                    def step(block, carry):
                        at = pl.ds(pl.multiple_of(block * 16, 16), 16)
                        put(
                            block,
                            entry(level, front, child, block - 2),
                            t_refs[level - 1][kid, at, :],
                            y_refs[level - 1][kid, at, :],
                        )
                        return carry

                    lax.fori_loop(2, 2 * group, step, 0, unroll=6)

            if level == 3:
                for half in range(2):
                    at = pl.ds(pl.multiple_of(half * BLOCK + 16 * s, 16), 16)
                    strip = top[at, :]
                    z_ref[0, 16 * half : 16 * half + 16, :] += strip
                    strip = jnp.where(p == 0, strip[:, :BLOCK], strip[:, BLOCK:])
                    strip = jnp.where(p < 2, strip, jnp.zeros_like(strip))
                    y_ref[0, 16 * half : 16 * half + 16, :BLOCK] += strip

            core_rows = (2, 3, 1) if level < 3 else (1,)
            if level == 1 and front == 0:
                for copy in copies[3:]:
                    copy.wait()
            if level == 1:
                kid_own = [[leaf_own(kid, q) for q in range(2)] for kid in kids]
                kid_core = [leaf_core(kid) for kid in kids]
            zt = []
            for q in range(wanted):
                parts = []
                own = jnp.zeros((BLOCK, 256), F32)
                for child, kid in enumerate(kids):
                    if level == 1:
                        value = kid_own[child][q % 2]
                    else:
                        value = own_refs[level - 1][kid, (q % 2) * BLOCK : (q % 2 + 1) * BLOCK, :]
                    own = own + masked(child, q, value.astype(F32))
                if level == 3:
                    strip = top[q * BLOCK : (q + 1) * BLOCK, :].astype(F32)
                    strip = jnp.where(p == 0, strip[:, :BLOCK], strip[:, BLOCK:])
                    strip = jnp.where(p < 2, strip, jnp.zeros_like(strip))
                    own = own + jnp.concatenate([strip, jnp.zeros_like(strip)], 1)
                parts.append(own)
                for r in core_rows:
                    value = jnp.zeros((BLOCK, BLOCK), F32)
                    for child, kid in enumerate(kids):
                        if level == 1:
                            part = kid_core[child][q % 2]
                        else:
                            part = core_refs[level - 1][kid, (q % 2) * BLOCK : (q % 2 + 1) * BLOCK, :]
                        part = part[:, (r % 2) * BLOCK : (r % 2 + 1) * BLOCK].astype(F32)
                        value = value + masked(child, q, masked(child, r, part))
                    if q == 0 and r == 1:
                        value = value + couplings[8 - (16 >> level) + front].astype(F32)
                    parts.append(value)
                zt.append(jnp.concatenate(parts, 1).astype(BF16))
            panels_t.append(zt)

        fronts = range(8 >> level)
        pieces = [(front, start) for front in fronts for start in range(0, width, CHUNK)]
        live = panels_t[0][0].shape[1] - BLOCK
        inverse = [
            [inverses[8 - (16 >> level) + front, q] for q in range(2)] for front in fronts
        ]

        def rows_of(ref, front, start, q):
            return ref[front, pl.ds(start, CHUNK), q * BLOCK : (q + 1) * BLOCK]

        scaled_zero_t = [dot(inverse[f][0], panels_t[f][0]).astype(BF16) for f in fronts]
        scaled_zero = [dot(rows_of(z_ref, f, at, 0), inverse[f][0]).astype(BF16) for f, at in pieces]
        second_t, second = [], []
        for f in fronts:
            coupling = panels_t[f][0][:, live:]
            value = panels_t[f][1].astype(F32) - dot_tn(coupling, scaled_zero_t[f])
            second_t.append(value.astype(BF16))
        for i, (f, at) in enumerate(pieces):
            coupling = panels_t[f][0][:, live:]
            value = rows_of(z_ref, f, at, 1).astype(F32) - dot(scaled_zero[i], coupling)
            second.append(value.astype(BF16))
        scaled_one_t = [dot(inverse[f][1], second_t[f]).astype(BF16) for f in fronts]
        if level < 3:
            scaled_one = [dot(second[i], inverse[f][1]).astype(BF16) for i, (f, _) in enumerate(pieces)]
            core_cols = [
                jnp.concatenate([panels_t[f][0][:, 256:512], second_t[f][:, 256:512]], 0)
                for f in fronts
            ]
            for f in fronts:
                later = jnp.concatenate([panels_t[f][2], panels_t[f][3]], 0)[:, :512].astype(F32)
                scaled = jnp.concatenate([scaled_zero_t[f][:, :512], scaled_one_t[f][:, :512]], 0)
                later = (later - dot_tn(core_cols[f], scaled)).astype(BF16)
                own_refs[level][f] = later[:, :256]
                core_refs[level][f] = later[:, 256:]
        for i, (f, at) in enumerate(pieces):
            own_scaled = jnp.concatenate([scaled_zero_t[f][:, :256], scaled_one_t[f][:, :256]], 0)
            columns = jnp.concatenate([rows_of(z_ref, f, at, 0), second[i]], 1)
            row = y_ref[f, pl.ds(at, CHUNK), :].astype(F32) - dot(columns, own_scaled)
            if level == 3:
                out[i] = row.T.astype(BF16)
                copy = pltpu.make_async_copy(
                    out.at[i], out_hbm.at[:, pl.ds(at, CHUNK)], left.at[i]
                )
                copy.start()
                copies.append(copy)
                continue
            y_ref[f, pl.ds(at, CHUNK), :] = row.astype(BF16)
            rest = z_ref[f, pl.ds(at, CHUNK), 2 * BLOCK :].astype(F32)
            rest = rest - dot(jnp.concatenate([scaled_zero[i], scaled_one[i]], 1), core_cols[f])
            t_refs[level][f, pl.ds(at, CHUNK), :] = rest.astype(BF16)
    for copy in copies[7:]:
        copy.wait()


def upper_levels(info, whole, got, near, other, pivots, inverses):
    anywhere = pl.BlockSpec(memory_space=pltpu.HBM)
    return pl.pallas_call(
        upper_kernel,
        out_shape=jax.ShapeDtypeStruct((256, 2048), BF16),
        in_specs=[pl.BlockSpec(memory_space=pltpu.SMEM)] + [pl.BlockSpec(memory_space=pl.ANY)] * 4 + [anywhere] * 2,
        out_specs=anywhere,
        scratch_shapes=[
            pltpu.VMEM(shape, BF16)
            for shape in (
                (4, 512, 512), (2, 1024, 512), (1, 2048, 256),
                (4, 512, 256), (2, 1024, 256), (1, 2048, 256),
                (4, 512, 256), (2, 1024, 256),
                (4, 256, 256), (2, 256, 256), (4, 256, 256), (2, 256, 256),
                (7, BLOCK, BLOCK), (256, 256), (7, 2, BLOCK, BLOCK),
                whole.shape, got.shape, near.shape, other.shape, (8, 256, CHUNK),
            )
        ]
        + [pltpu.SemaphoreType.DMA((7,)), pltpu.SemaphoreType.DMA((8,))],
        compiler_params=pltpu.CompilerParams(vmem_limit_bytes=62 * 2**20),
        name="upper_levels",
    )(info, whole, got, near, other, pivots, inverses)


def leaf_stage(leaf, inverses, zl, xl, c, u):
    tile = leaf
    spread = jnp.where(xl == 0, tile, lax.ppermute(tile, "xl", [(0, 1)]))
    spread = jnp.where(zl == 0, spread, lax.ppermute(spread, "zl", [(0, 1)]))
    other = lax.ppermute(spread, "c", [(0, 1), (1, 0)])
    even = jnp.where(c == 0, spread, other)
    odd = jnp.where(c == 0, other, spread)
    piece = jnp.concatenate(
        [
            tile[:, :32],
            odd[:BLOCK, :32],
            even[BLOCK:, :32],
            odd[BLOCK:, :32],
            even[BLOCK:, 128:160],
            odd[BLOCK:, 128:160],
        ],
        0,
    ).T
    got = lax.all_to_all(jnp.broadcast_to(piece[None], (8,) + piece.shape), "sub", 0, 0, tiled=True)
    got = got.reshape(8, 2, 16, 896).transpose(1, 0, 2, 3).reshape(2, BLOCK, 896)
    first = jnp.concatenate([even[:BLOCK], got[0, :, :640]], 1)
    second = jnp.concatenate([odd[:BLOCK], got[1, :, :640]], 1)
    columns, scaled = panels(first, second, inverses[0], inverses[1], 512)
    core = got[:, :, 640:].reshape(256, 256).astype(F32)
    core = core - dot_tn(columns[:, 640:], scaled[:, 640:])
    core = core.astype(BF16)
    upper = lax.dynamic_slice_in_dim(core[:BLOCK], 16 * u, 16, 0)
    lower = lax.dynamic_slice_in_dim(core[BLOCK:, BLOCK:], 16 * u, 16, 0)
    tile = tile.T.astype(F32) - dot_tn(columns[:, :256], scaled[:, 256:512])
    return jnp.concatenate(
        [tile[32:].astype(BF16), upper, jnp.concatenate([lower[:8], lower[8:]], 1)], 0
    )


def local(leaf_fronts, pivot_entries, pivot_inverse, block_map_one, block_map_two, block_map_top):
    k, zl, xl, c = (lax.axis_index(name) for name in ("k", "zl", "xl", "c"))
    s = lax.axis_index("sub")
    u = zl * 4 + xl * 2 + c
    maps = (block_map_one, block_map_two, block_map_top)
    info = jnp.concatenate(
        [jnp.stack([k * 8 + u, s, u]).astype(jnp.int32)] + [table.reshape(-1) for table in maps]
    )
    payload = leaf_stage(
        leaf_fronts, lax.dynamic_index_in_dim(pivot_inverse, k, 0, keepdims=False), zl, xl, c, u
    )
    whole = lax.all_gather(payload, "k")
    piece = jnp.concatenate([whole[:, 96:112], whole[:, 112:128]], 2)
    got = lax.all_to_all(jnp.broadcast_to(piece[None], (8, 8, 16, 512)), "sub", 0, 0, tiled=True)
    core = jnp.concatenate(
        [
            whole[:, 224:240, :BLOCK],
            whole[:, 224:240, BLOCK:],
            whole[:, 240:, :BLOCK],
            whole[:, 240:, BLOCK:],
        ],
        1,
    ).reshape(384, BLOCK)
    columns = whole[:, :224, BLOCK:].reshape(CORE_AT, BLOCK)
    first, second = columns[:SPLIT], columns[SPLIT:]
    down, swap = [(0, 1)], [(0, 1), (1, 0)]
    far = lax.ppermute(jnp.concatenate([first, core], 0), "xl", swap)
    one = jnp.where(xl == 0, first, far[:SPLIT])
    two = jnp.where(zl == 0, second, lax.ppermute(second, "zl", down))
    cores = jnp.concatenate([core, far[SPLIT:]], 0)
    far = lax.ppermute(jnp.concatenate([one, cores], 0), "zl", swap)
    one = jnp.where(zl == 0, one, far[:SPLIT])
    two = jnp.where(xl == 0, two, lax.ppermute(two, "xl", down))
    near = jnp.concatenate([one, two, cores, far[SPLIT:]], 0)
    other = lax.ppermute(near, "c", swap)
    return upper_levels(info, whole, got, near, other, pivot_entries, pivot_inverse)


def solution(mesh):
    cube = ("k", "zl", "xl", "c")
    split = Mesh(mesh.devices.reshape(8, 2, 2, 2, 8), cube + ("sub",))
    return jax.shard_map(
        local,
        mesh=split,
        in_specs=(P(cube, "sub"), P(), P(), P(), P(), P()),
        out_specs=P(cube, "sub"),
        check_vma=False,
    )
```
